128 devices in a mesh: seq: 32 (over x, z, core), wt: 4 (over y).
Axes of the slice: x: 4, y: 4, z: 4, core: 2. Of those that a mesh axis runs over, the one named last changes fastest.
Arguments:
- tokens: bfloat16 [4, 8192, 768], P('wt', 'seq'), may hold values from -6 to 6
- in_w: float32 [2, 768, 3352], P(None, 'wt'), may hold values from -0.21875 to 0.21875
- in_m: float32 [2, 768, 3352], P(None, 'wt'), may hold values from -64 to 64
- in_v: float32 [2, 768, 3352], P(None, 'wt'), may hold values from 218.56256 to 3276.8
- out_w: float32 [2, 1536, 768], P(None, 'wt'), may hold values from -0.15625 to 0.15625
- out_m: float32 [2, 1536, 768], P(None, 'wt'), may hold values from -64 to 64
- out_v: float32 [2, 1536, 768], P(None, 'wt'), may hold values from 218.56256 to 3276.8
- small_params: float32 [2, 11336], P(None, 'wt'), as said below
- small_m: float32 [2, 11336], P(None, 'wt'), may hold values from -64 to 64
- small_v: float32 [2, 11336], P(None, 'wt'), may hold values from 218.56256 to 3276.8
- cotangent: bfloat16 [4, 8192, 768], P('wt', 'seq'), may hold values from -6 to 6
Outputs:
- layer_out: float32 [4, 8192, 768], P('wt', 'seq')
- input_grad: float32 [4, 8192, 768], P('wt', 'seq')
- new_in_m: float32 [2, 768, 3352], P(None, 'wt')
- new_in_v: float32 [2, 768, 3352], P(None, 'wt')
- new_in_w: float32 [2, 768, 3352], P(None, 'wt')
- new_out_m: float32 [2, 1536, 768], P(None, 'wt')
- new_out_v: float32 [2, 1536, 768], P(None, 'wt')
- new_out_w: float32 [2, 1536, 768], P(None, 'wt')
- new_small_m: float32 [2, 11336], P(None, 'wt')
- new_small_v: float32 [2, 11336], P(None, 'wt')
- new_small: float32 [2, 11336], P(None, 'wt')
The draws below stay inside these ranges and needn't reach their ends.
Inputs may be any that keep to these rules, and one draw needn't show every extreme that they name: `small_params`: each row is one layer: gains near one, convolution taps of both signs, decay logarithms between log(1.6 / 8192) and log(0.17), step biases between -1.5 and -0.5, skip gains between 0.5 and 1.5.
All inputs are finite; a program needn't handle non-finite values.
Results may differ from the reference program's by a relative error of at most 0.019.
The reference program's roundings to bfloat16 on the way count: a program that leaves them out, or rounds other values in their place, can miss the bound.
Values may be sent and summed in bfloat16 or wider, within the bound.
No kernel may reach another device: no remote copies, remote signals or barrier semaphores. Data moves between devices by JAX's collectives and lax.ppermute only.
A program may use at most 320 MiB of HBM per device.

```python
import math
import jax
import jax.numpy as jnp
from jax import lax

D = 768
HEADS = 24
HDIM = 64
NSTATE = 128
WIDTH = 4
LAYERS = 2
STEP = 10
INNER = 1536
CONV = 1792
PROJ = 3352
VEC = 11336
LENGTH = 8192
SEQS = 4
TOKENS = 32768


def draw_small_params(key, part):
    key = jax.random.fold_in(key, 7)
    subkeys = jax.random.split(key, 9)
    gain_in = jax.random.uniform(subkeys[0], (LAYERS, D), jnp.float32, 0.6, 1.4)
    gain_out = jax.random.uniform(subkeys[1], (LAYERS, INNER), jnp.float32, 0.6, 1.4)
    conv_taps = jnp.clip(0.5 * jax.random.normal(subkeys[2], (LAYERS, WIDTH * CONV), jnp.float32), -2.0, 2.0)
    slow_share = 0.5
    conv_bias = jnp.clip(0.3 * jax.random.normal(subkeys[3], (LAYERS, CONV), jnp.float32), -1.0, 1.0)
    slow_heads = jax.random.uniform(subkeys[4], (LAYERS, HEADS), jnp.float32) < slow_share
    slow_rate = jnp.exp(jax.random.uniform(subkeys[5], (LAYERS, HEADS), jnp.float32, math.log(0.5 / LENGTH), math.log(2.0 / LENGTH)))
    fast_rate = jnp.exp(jax.random.uniform(subkeys[6], (LAYERS, HEADS), jnp.float32, math.log(0.02), math.log(0.05)))
    decay_log = jnp.log(jnp.where(slow_heads, slow_rate, fast_rate) / 0.3)
    dt_bias = jax.random.uniform(subkeys[7], (LAYERS, HEADS), jnp.float32, -1.5, -0.5)
    skip_gain = jax.random.uniform(subkeys[8], (LAYERS, HEADS), jnp.float32, 0.5, 1.5)
    return jnp.concatenate([gain_in, gain_out, conv_taps, conv_bias, decay_log, dt_bias, skip_gain], axis=1)


def steps_of(stream_key, shape, cuts, smallest, top_value):
    level, own = 1.0, jax.random.fold_in(stream_key, 6)
    for dim, blocks in cuts:
        steps = jnp.exp(jax.random.uniform(jax.random.fold_in(own, dim), (blocks,), jnp.float32, smallest / len(cuts), top_value / len(cuts)))
        level = level * jnp.repeat(steps, shape[dim] // blocks).reshape([-1 if axis == dim else 1 for axis in range(len(shape))])
    return level


def gaussian(key, dims, spread, most, cuts=(), held_as=jnp.bfloat16):
    loudness = steps_of(key, dims, cuts, -0.22, 0.18) if cuts else 1.0
    drawn = jax.random.normal(key, dims, jnp.float32) * spread * loudness
    return jnp.minimum(jnp.maximum(drawn, -most), most).astype(held_as)


def setup_inputs(seed: int = 0) -> dict:
    seeds = jax.random.split(jax.random.key(seed), 12)
    return {
        "tokens": gaussian(seeds[0], (SEQS, LENGTH, D), 1.0, 6.0, ((0, 4), (1, 32))),
        "in_w": gaussian(seeds[1], (LAYERS, D, PROJ), D ** -0.5, 0.21875, ((1, 4),), jnp.float32),
        "in_m": gaussian(seeds[2], (LAYERS, D, PROJ), (TOKENS ** 0.5 * 324 ** -0.5), 64.0, ((1, 4),), jnp.float32),
        "in_v": jnp.clip(jnp.exp(math.log(3276.8) - 2.7075503 * jax.random.uniform(seeds[3], (LAYERS, D, PROJ), jnp.float32) ** steps_of(seeds[3], (LAYERS, D, PROJ), ((1, 4),), -0.2, 0.2)), 218.56256, 3276.8),
        "out_w": gaussian(seeds[4], (LAYERS, INNER, D), INNER ** -0.5, 0.15625, ((1, 4),), jnp.float32),
        "out_m": gaussian(seeds[5], (LAYERS, INNER, D), (TOKENS ** 0.5 * 324 ** -0.5), 64.0, ((1, 4),), jnp.float32),
        "out_v": jnp.clip(jnp.exp(math.log(3276.8) - 2.7075503 * jax.random.uniform(seeds[6], (LAYERS, INNER, D), jnp.float32) ** steps_of(seeds[6], (LAYERS, INNER, D), ((1, 4),), -0.2, 0.2)), 218.56256, 3276.8),
        "small_params": draw_small_params(jax.random.fold_in(seeds[11], 71), 0),
        "small_m": gaussian(seeds[8], (LAYERS, VEC), (TOKENS ** 0.5 * 324 ** -0.5), 64.0, ((1, 4),), jnp.float32),
        "small_v": jnp.clip(jnp.exp(math.log(3276.8) - 2.7075503 * jax.random.uniform(seeds[9], (LAYERS, VEC), jnp.float32) ** steps_of(seeds[9], (LAYERS, VEC), ((1, 4),), -0.2, 0.2)), 218.56256, 3276.8),
        "cotangent": gaussian(seeds[10], (SEQS, LENGTH, D), 1.0, 6.0, ((0, 4), (1, 32))),
    }


@jax.custom_vjp
def low(v):
    return lax.optimization_barrier(v.astype(jnp.bfloat16)).astype(jnp.float32)

@jax.custom_vjp
def low_back(v):
    return v

def low_keep(v):
    return (low(v), None)

def low_pass(kept, grad):
    return (grad,)

def back_keep(v):
    return (v, None)

def back_low(kept, grad):
    return (low(grad),)
low.defvjp(low_keep, low_pass)
low_back.defvjp(back_keep, back_low)
highest = lax.Precision.HIGHEST

def rms_scale(values, gain_values):
    return values * lax.rsqrt(lax.optimization_barrier(jnp.mean(values * values, axis=-1, keepdims=True)) + 1e-05) * gain_values

def split_params(params):
    gain_in = params[0:D]
    gain_out = params[D:D + INNER]
    offset = D + INNER
    conv_taps = params[offset:offset + WIDTH * CONV].reshape(WIDTH, CONV)
    offset = offset + WIDTH * CONV
    conv_bias = params[offset:offset + CONV]
    offset = offset + CONV
    decay_log = params[offset:offset + HEADS]
    dt_bias = params[offset + HEADS:offset + 2 * HEADS]
    skip_gain = params[offset + 2 * HEADS:offset + 3 * HEADS]
    return (gain_in, gain_out, conv_taps, conv_bias, decay_log, dt_bias, skip_gain)

def prepare(projected, edge_rows, params):
    param_parts = split_params(params)
    conv_taps = param_parts[2]
    row_count = projected.shape[0]
    z_part = projected[:, :INNER]
    conv_in = projected[:, INNER:INNER + CONV]
    dt_raw = projected[:, INNER + CONV:]
    padded = jnp.concatenate([edge_rows, conv_in], axis=0)
    conv_sum = param_parts[3][None, :] + conv_taps[0][None, :] * padded[0:row_count]
    for offset in range(1, WIDTH):
        conv_sum = conv_sum + conv_taps[offset][None, :] * padded[offset:offset + row_count]
    conv_out = jax.nn.silu(conv_sum)
    x_heads = conv_out[:, :INNER].reshape(row_count, HEADS, HDIM)
    b_proj = conv_out[:, INNER:INNER + NSTATE]
    c_proj = conv_out[:, INNER + NSTATE:]
    step_size = jax.nn.softplus(dt_raw + param_parts[5][None, :])
    log_decay = -step_size * jnp.exp(param_parts[4])[None, :]
    return (z_part, x_heads, b_proj, c_proj, log_decay, step_size)

def scan_blocks(x_heads, b_proj, c_proj, log_decay, step_size, block_rows):
    row_count = x_heads.shape[0]
    block_count = row_count // block_rows
    pieces = (x_heads.reshape(block_count, block_rows, HEADS, HDIM), b_proj.reshape(block_count, block_rows, NSTATE), c_proj.reshape(block_count, block_rows, NSTATE), log_decay.reshape(block_count, block_rows, HEADS), step_size.reshape(block_count, block_rows, HEADS))
    causal = jnp.arange(block_rows)[:, None] >= jnp.arange(block_rows)[None, :]

    def one_block(states, piece_set):
        heads_block, b_block, c_block, decay_block, step_block = piece_set
        cum_decay = jnp.cumsum(decay_block, axis=0)
        cum_heads = cum_decay.T
        pair_diff = cum_heads[:, :, None] - cum_heads[:, None, :]
        decay_pairs = jnp.exp(jnp.where(causal[None], pair_diff, -1e+30))
        scores = jnp.dot(c_block, b_block.T, precision=highest)
        weight_mat = decay_pairs * scores[None] * step_block.T[:, None, :]
        within = jnp.einsum('hij,jhp->ihp', weight_mat, heads_block, precision=highest)
        carried = jnp.einsum('in,hpn->ihp', c_block, states, precision=highest) * jnp.exp(cum_decay)[:, :, None]
        tail_weight = jnp.exp(cum_decay[-1:] - cum_decay) * step_block
        new_states = jnp.exp(cum_decay[-1])[:, None, None] * states + jnp.einsum('jh,jhp,jn->hpn', tail_weight, heads_block, b_block, precision=highest)
        return (new_states, within + carried)
    final_states, outputs = lax.scan(jax.checkpoint(one_block), jnp.zeros((HEADS, HDIM, NSTATE), jnp.float32), pieces)
    return (outputs.reshape(row_count, HEADS, HDIM), final_states)

def gate_out(ssm_heads, z_part, x_heads, params):
    param_parts = split_params(params)
    with_skip = ssm_heads + param_parts[6][None, :, None] * x_heads
    flat_out = with_skip.reshape(z_part.shape[0], INNER)
    return rms_scale(flat_out * jax.nn.silu(z_part), param_parts[1])

def layer_stack(sequence, in_low, out_low, small_low):
    block_rows = math.gcd(LENGTH, 256)
    hidden_rows = sequence
    for layer_index in range(LAYERS):
        params = small_low[layer_index]
        normed = low(rms_scale(hidden_rows, params[:D]))
        projected = low_back(jnp.dot(normed, in_low[layer_index], precision=highest))
        edge_rows = jnp.zeros((WIDTH - 1, CONV), jnp.float32)
        z_part, x_heads, b_proj, c_proj, log_decay, step_size = prepare(projected, edge_rows, params)
        ssm_heads, final_states = scan_blocks(x_heads, b_proj, c_proj, log_decay, step_size, block_rows)
        gated = low(gate_out(ssm_heads, z_part, x_heads, params))
        branch = low_back(jnp.dot(gated, out_low[layer_index], precision=highest))
        hidden_rows = hidden_rows + branch
    return hidden_rows

def adam_step(weight, moment, second, gradient, learn_rate, weight_decay):
    new_moment = 0.9 * moment + 0.1 * gradient
    new_second = 0.95 * second + 0.05 * gradient * gradient
    corrected = new_moment / (1.0 - 0.9 ** STEP) / (jnp.sqrt(new_second / (1.0 - 0.95 ** STEP)) + 1e-08)
    return (new_moment, new_second, weight - learn_rate * (corrected + weight_decay * weight))

def reference(tokens, in_w, in_m, in_v, out_w, out_m, out_v, small_params, small_m, small_v, cotangent):

    def forward(all_tokens, in_weight, out_weight, small_weight):
        in_low = low(in_weight)
        out_low = low(out_weight)
        small_low = low(small_weight)

        def one_sequence(sequence):
            return layer_stack(sequence, in_low, out_low, small_low)
        return lax.map(one_sequence, all_tokens)
    layer_out, pullback = jax.vjp(forward, tokens.astype(jnp.float32), in_w, out_w, small_params)
    input_grad, in_total, out_total, small_total = pullback(cotangent.astype(jnp.float32))
    new_in_m, new_in_v, new_in_w = adam_step(in_w, in_m, in_v, in_total, 0.03, 0.1)
    new_out_m, new_out_v, new_out_w = adam_step(out_w, out_m, out_v, out_total, 0.02, 0.1)
    new_small_m, new_small_v, new_small = adam_step(small_params, small_m, small_v, small_total, 0.2, 0.0)
    return (layer_out, input_grad, new_in_m, new_in_v, new_in_w, new_out_m, new_out_v, new_out_w, new_small_m, new_small_v, new_small)
```

```python
import functools

import jax
import jax.numpy as jnp
from jax import lax
from jax.experimental import pallas as pl
from jax.experimental.pallas import tpu as pltpu
from jax.sharding import Mesh
from jax.sharding import PartitionSpec as P

D = 768
HEADS = 24
HDIM = 64
NSTATE = 128
WIDTH = 4
STEP = 10
INNER = 1536
CONV = 1792
PROJ = 3352
VEC = 11336
ROWS = 256
EPS = 1e-05
PAIRS = HEADS // 2
LANES = 128
PLANE = ("x", "z", "core")

bf16 = jnp.bfloat16
f32 = jnp.float32
VMEM_BYTES = 48 * 1024 * 1024


def call(kernel, outs, scratch=(), grid=(), in_specs=None, out_specs=None, flops=0, moved=0, **kw):
    params = pltpu.CompilerParams(vmem_limit_bytes=VMEM_BYTES)
    extra = {}
    if in_specs is not None:
        extra["in_specs"] = in_specs
        extra["out_specs"] = out_specs
    return pl.pallas_call(
        kernel,
        out_shape=outs,
        grid=grid,
        scratch_shapes=list(scratch),
        compiler_params=params,
        cost_estimate=pl.CostEstimate(flops=flops, bytes_accessed=moved, transcendentals=0),
        **extra,
        **kw,
    )


def sds(shape, dtype):
    return jax.ShapeDtypeStruct(shape, dtype)


def dot(a, b):
    return lax.dot_general(a, b, (((1,), (0,)), ((), ())), preferred_element_type=f32)


def dot_nt(a, b):
    return lax.dot_general(a, b, (((1,), (1,)), ((), ())), preferred_element_type=f32)


def dot_tn(a, b):
    return lax.dot_general(a, b, (((0,), (0,)), ((), ())), preferred_element_type=f32)


def split2(v):
    high = v.astype(bf16)
    return high, (v - high.astype(f32)).astype(bf16)


def split3(v):
    high = v.astype(bf16)
    rest = v - high.astype(f32)
    mid = rest.astype(bf16)
    return high, mid, (rest - mid.astype(f32)).astype(bf16)


def iota(shape, dim):
    return lax.broadcasted_iota(jnp.int32, shape, dim)


def sigmoid(v):
    return 1.0 / (1.0 + jnp.exp(-v))


def softplus(v):
    return jnp.maximum(v, 0.0) + jnp.log1p(jnp.exp(-jnp.abs(v)))


def pair_of(v, p):
    rows = v.shape[0]
    left = jnp.broadcast_to(v[:, 2 * p : 2 * p + 1], (rows, LANES))
    right = jnp.broadcast_to(v[:, 2 * p + 1 : 2 * p + 2], (rows, LANES))
    return jnp.where(iota((rows, LANES), 1) < HDIM, left, right)


def head_mask(columns, first_head):
    return ((iota((columns, LANES), 0) >> 6) + first_head == iota((columns, LANES), 1)).astype(bf16)


def running_sum(v, reverse):
    rows, cols = iota((ROWS, ROWS), 0), iota((ROWS, ROWS), 1)
    tri = ((cols >= rows) if reverse else (cols <= rows)).astype(bf16)
    high, mid, low = split3(v)
    return dot(tri, high) + dot(tri, mid) + dot(tri, low)


def project_kernel(x_ref, gain_ref, w_ref, normed_ref, proj_ref):
    @pl.when(pl.program_id(0) == 0)
    def _():
        x = x_ref[...].astype(f32)
        scale = lax.rsqrt(jnp.mean(x * x, axis=-1, keepdims=True) + EPS)
        normed_ref[...] = (x * scale * gain_ref[...]).astype(bf16)

    proj_ref[...] = dot(normed_ref[...], w_ref[...])


def project(x, gain, weight):
    block = 512
    return call(
        project_kernel,
        (sds((ROWS, D), bf16), sds((ROWS, PROJ), f32)),
        grid=(pl.cdiv(PROJ, block),),
        in_specs=[
            pl.BlockSpec((ROWS, D), lambda k: (0, 0)),
            pl.BlockSpec((1, D), lambda k: (0, 0)),
            pl.BlockSpec((D, block), lambda k: (0, k)),
        ],
        out_specs=[
            pl.BlockSpec((ROWS, D), lambda k: (0, 0)),
            pl.BlockSpec((ROWS, block), lambda k: (0, k)),
        ],
        flops=2 * ROWS * D * PROJ,
        moved=9_500_000,
        name="project",
    )(x, gain, weight)


def conv_kernel(
    edge_ref, gain_ref, w_ref, proj_ref, dt_ref, taps_ref, bias_ref, decay_ref, dtb_ref,
    pre_ref, edge_out_ref, vbc_ref, cum_ref, step_ref, pay_ref,
    edge_n, ext, b_keep, tail_keep, states,
):
    k = pl.program_id(0)

    @pl.when(k == 0)
    def _():
        edge = edge_ref[...].astype(f32)
        scale = lax.rsqrt(jnp.mean(edge * edge, axis=-1, keepdims=True) + EPS)
        edge_n[0:8] = edge * scale * gain_ref[...]
        edge_n[8:16] = jnp.zeros((8, D), f32)
        inside = iota((ROWS, LANES), 1) < HEADS
        raw = jnp.where(inside, dt_ref[...], 0.0)
        step = jnp.where(inside, softplus(raw + dtb_ref[...]), 0.0)
        cum = running_sum(-step * jnp.exp(decay_ref[...]), False)
        step_ref[...] = step
        cum_ref[...] = cum
        tail_keep[...] = jnp.exp(cum[ROWS - 1 : ROWS] - cum)

    edge_in = dot(edge_n[...].astype(bf16), w_ref[...])[0:8]
    edge_out_ref[...] = edge_in
    ext[0:8] = edge_in
    ext[8 : 8 + ROWS] = proj_ref[...]
    total = bias_ref[...] + taps_ref[0:1] * ext[5 : 5 + ROWS]
    for tap in range(1, WIDTH):
        total = total + taps_ref[tap : tap + 1] * ext[5 + tap : 5 + tap + ROWS]
    pre_ref[...] = total
    out = total * sigmoid(total)

    @pl.when(k == 0)
    def _():
        vbc_ref[...] = out.astype(bf16)
        b_keep[...] = out[:, :NSTATE].astype(bf16)

    @pl.when(k > 0)
    def _():
        mask = head_mask(256, 4 * (k - 1))
        s_high, s_low = split2(step_ref[...])
        value = out * (dot_nt(s_high, mask) + dot_nt(s_low, mask))
        vbc_ref[...] = value.astype(bf16)
        t_high, t_low = split2(tail_keep[...])
        tailed = value * (dot_nt(t_high, mask) + dot_nt(t_low, mask))
        row = pl.multiple_of((k - 1) * 256, 256)
        states[pl.ds(row, 256), :] = dot_tn(tailed.astype(bf16), b_keep[...])

    @pl.when(k == 6)
    def _():
        total_log = cum_ref[ROWS - 1 : ROWS, :]
        piece = iota((32, LANES), 0)
        head = (piece * 48 + iota((32, LANES), 1)) >> 6
        logs = jnp.zeros((32, LANES), f32)
        for h in range(HEADS):
            logs = jnp.where(head == h, total_log[:, h : h + 1], logs)
        row16 = iota((16, LANES), 0)
        for piece in range(32):
            pay_ref[piece, 0:48, :] = states[48 * piece : 48 * piece + 48, :].astype(bf16)
            line = logs[piece : piece + 1, :]
            high = line.astype(bf16).astype(f32)
            extra = jnp.where(row16 == 0, high, jnp.where(row16 == 1, line - high, 0.0))
            pay_ref[piece, 48:64, :] = extra.astype(bf16)


def conv_states(edge, gain, weight, proj, taps, bias, decay, dtb):
    block = 256
    turn = lambda k: (k + 6) % 7
    whole = lambda k: (0, 0)
    return call(
        conv_kernel,
        (
            sds((ROWS, CONV), f32),
            sds((8, CONV), f32),
            sds((ROWS, CONV), bf16),
            sds((ROWS, LANES), f32),
            sds((ROWS, LANES), f32),
            sds((32, 64, LANES), bf16),
        ),
        scratch=[
            pltpu.VMEM((16, D), f32),
            pltpu.VMEM((ROWS + 8, block), f32),
            pltpu.VMEM((ROWS, NSTATE), bf16),
            pltpu.VMEM((ROWS, LANES), f32),
            pltpu.VMEM((INNER, NSTATE), f32),
        ],
        grid=(7,),
        in_specs=[
            pl.BlockSpec((8, D), whole),
            pl.BlockSpec((1, D), whole),
            pl.BlockSpec((D, block), lambda k: (0, 6 + turn(k))),
            pl.BlockSpec((ROWS, block), lambda k: (0, 6 + turn(k))),
            pl.BlockSpec((ROWS, LANES), lambda k: (0, 26)),
            pl.BlockSpec((WIDTH, block), lambda k: (0, turn(k))),
            pl.BlockSpec((1, block), lambda k: (0, turn(k))),
            pl.BlockSpec((1, LANES), whole),
            pl.BlockSpec((1, LANES), whole),
        ],
        out_specs=[
            pl.BlockSpec((ROWS, block), lambda k: (0, turn(k))),
            pl.BlockSpec((8, block), lambda k: (0, turn(k))),
            pl.BlockSpec((ROWS, block), lambda k: (0, turn(k))),
            pl.BlockSpec((ROWS, LANES), whole),
            pl.BlockSpec((ROWS, LANES), whole),
            pl.BlockSpec((32, 64, LANES), lambda k: (0, 0, 0)),
        ],
        flops=2 * ROWS * INNER * NSTATE + 2 * 16 * D * CONV,
        moved=9_000_000,
        name="conv_states",
    )(edge, gain, weight, proj, proj, taps, bias, decay, dtb)


def within_kernel(vbc_ref, cum_ref, y_ref, score):
    b_part = vbc_ref[:, INNER : INNER + NSTATE]
    c_part = vbc_ref[:, INNER + NSTATE :]
    keep = iota((ROWS, ROWS), 0) >= iota((ROWS, ROWS), 1)
    score[...] = jnp.where(keep, dot_nt(c_part, b_part), 0.0)
    cum = cum_ref[...]
    cum_t = jnp.transpose(cum)
    left = iota((LANES, LANES), 1) < HDIM
    for p in range(PAIRS):
        values = vbc_ref[:, p * LANES : (p + 1) * LANES]
        tops, lows = [], []
        for h in (2 * p, 2 * p + 1):
            col, row = cum[:, h : h + 1], cum_t[h : h + 1, :]
            top = jnp.exp(jnp.minimum(col[0:LANES] - row[:, 0:LANES], 0.0)) * score[0:LANES, 0:LANES]
            tops.append(dot(top.astype(bf16), values[0:LANES]))
            low = jnp.exp(jnp.minimum(col[LANES:] - row, 0.0)) * score[LANES:, :]
            lows.append(dot(low.astype(bf16), values))
        y_ref[0:LANES, p * LANES : (p + 1) * LANES] = jnp.where(left, tops[0], tops[1])
        y_ref[LANES:, p * LANES : (p + 1) * LANES] = jnp.where(left, lows[0], lows[1])


def within(vbc, cum):
    return call(
        within_kernel,
        sds((ROWS, INNER), f32),
        scratch=[pltpu.VMEM((ROWS, ROWS), f32)],
        flops=2 * HEADS * ROWS * ROWS * LANES * 4,
        moved=3_000_000,
        name="within",
    )(vbc, cum)


def scan_kernel(pay_ref, out_ref, decay_ref, logs):
    logs[...] = jnp.zeros_like(logs)
    for s in range(32):
        extra = pay_ref[s, 48:64, :].astype(f32)
        logs[s : s + 1, :] = extra[0:1] + extra[1:2]
    decay = jnp.exp(jnp.transpose(logs[...]))
    decay_ref[...] = decay
    carry = jnp.zeros((48, LANES), f32)
    for s in range(32):
        out_ref[s] = carry.astype(bf16)
        carry = decay[0:48, s : s + 1] * carry + pay_ref[s, 0:48, :].astype(f32)


def scan_states(pay):
    return call(
        scan_kernel,
        (sds((32, 48, LANES), bf16), sds((LANES, LANES), f32)),
        scratch=[pltpu.VMEM((LANES, LANES), f32)],
        moved=1_000_000,
        name="scan_states",
    )(pay)


def scan_back_kernel(grad_ref, decay_ref, out_ref):
    decay = decay_ref[...]
    carry = jnp.zeros((48, LANES), f32)
    for s in reversed(range(32)):
        out_ref[s] = carry.astype(bf16)
        carry = decay[0:48, s : s + 1] * carry + grad_ref[s].astype(f32)


def scan_back(grad, decay):
    return call(
        scan_back_kernel, sds((32, 48, LANES), bf16), moved=800_000, name="scan_back"
    )(grad, decay)


def output_kernel(
    yw_ref, c_ref, cum_ref, pre_ref, z_ref, state_ref, hid_ref, w_ref, gain_ref, skip_ref,
    hid_out, y_out, gated_ref, gate,
):
    grown = jnp.exp(cum_ref[...])
    c_part = c_ref[...]
    rows = hid_ref.shape[0]
    square = jnp.zeros((rows, 1), f32)
    for p in range(PAIRS):
        cols = slice(p * LANES, (p + 1) * LANES)
        y = yw_ref[:, cols] + dot_nt(c_part, state_ref[cols, :]) * pair_of(grown, p)
        y_out[:, cols] = y
        pre = pre_ref[:, cols]
        z = z_ref[:, cols]
        u = (y + skip_ref[:, cols] * (pre * sigmoid(pre))) * (z * sigmoid(z))
        gate[:, cols] = u
        square = square + jnp.sum(u * u, axis=-1, keepdims=True)
    scale = lax.rsqrt(square * (1.0 / INNER) + EPS)
    gated_ref[...] = (gate[...] * scale * gain_ref[...]).astype(bf16)
    hid_out[...] = hid_ref[...].astype(f32) + dot(gated_ref[...], w_ref[...])


def output_part(yw, vbc, cum, pre, proj, states, hidden, weight, gain, skip):
    rows = 128
    take = lambda k: (k, 0)
    whole = lambda k: (0, 0)
    return call(
        output_kernel,
        (sds((ROWS, D), f32), sds((ROWS, INNER), f32), sds((ROWS, INNER), bf16)),
        scratch=[pltpu.VMEM((rows, INNER), f32)],
        grid=(ROWS // rows,),
        in_specs=[
            pl.BlockSpec((rows, INNER), take),
            pl.BlockSpec((rows, LANES), lambda k: (k, 13)),
            pl.BlockSpec((rows, LANES), take),
            pl.BlockSpec((rows, INNER), take),
            pl.BlockSpec((rows, INNER), take),
            pl.BlockSpec((INNER, LANES), whole),
            pl.BlockSpec((rows, D), take),
            pl.BlockSpec((INNER, D), whole),
            pl.BlockSpec((1, INNER), whole),
            pl.BlockSpec((1, INNER), whole),
        ],
        out_specs=[
            pl.BlockSpec((rows, D), take),
            pl.BlockSpec((rows, INNER), take),
            pl.BlockSpec((rows, INNER), take),
        ],
        flops=2 * ROWS * INNER * (D + LANES),
        moved=10_000_000,
        name="output_part",
    )(yw, vbc, cum, pre, proj, states, hidden, weight, gain, skip)


def gate_back_kernel(
    grad_ref, w_ref, y_ref, z_ref, pre_ref, c_ref, cum_ref, gain_ref, skip_ref,
    low_ref, dz_ref, dy_ref, local_ref, row_ref, dgain_ref, dskip_ref,
    gate, back, high, low, heads,
):
    low_ref[...] = grad_ref[...].astype(bf16)
    back[...] = dot_nt(low_ref[...], w_ref[...])
    square = jnp.zeros((ROWS, 1), f32)
    cross = jnp.zeros((ROWS, 1), f32)
    for p in range(PAIRS):
        cols = slice(p * LANES, (p + 1) * LANES)
        pre, z = pre_ref[:, cols], z_ref[:, cols]
        u = (y_ref[:, cols] + skip_ref[:, cols] * (pre * sigmoid(pre))) * (z * sigmoid(z))
        gate[:, cols] = u
        square = square + jnp.sum(u * u, axis=-1, keepdims=True)
        cross = cross + jnp.sum(back[:, cols] * gain_ref[:, cols] * u, axis=-1, keepdims=True)
    scale = lax.rsqrt(square * (1.0 / INNER) + EPS)
    pull = scale * scale * scale * cross * (1.0 / INNER)
    grown = jnp.exp(cum_ref[...])
    for p in range(PAIRS):
        cols = slice(p * LANES, (p + 1) * LANES)
        pre, z, y = pre_ref[:, cols], z_ref[:, cols], y_ref[:, cols]
        u, grad = gate[:, cols], back[:, cols]
        x = pre * sigmoid(pre)
        dgain_ref[:, cols] = jnp.sum(grad * u * scale, axis=0, keepdims=True)
        du = grad * gain_ref[:, cols] * scale - u * pull
        sig = sigmoid(z)
        dssm = du * (z * sig)
        ssm = y + skip_ref[:, cols] * x
        dz_ref[:, cols] = (du * ssm * (sig * (1.0 + z * (1.0 - sig)))).astype(bf16)
        dy = dssm.astype(bf16)
        dy_ref[:, cols] = dy
        gate[0:1, cols] = jnp.sum(dssm * x, axis=0, keepdims=True)
        a, b = split2(dy.astype(f32) * y)
        high[:, cols] = a
        low[:, cols] = b
        heads[:, cols] = (dssm * pair_of(grown, p)).astype(bf16)
    mask = head_mask(INNER, 0)
    row_ref[...] = dot(high[...], mask) + dot(low[...], mask)
    a, b = split2(jnp.broadcast_to(gate[0:1, :], (16, INNER)))
    dskip_ref[...] = (dot(a, mask) + dot(b, mask))[0:8]
    for part in range(4):
        cols = slice(384 * part, 384 * part + 384)
        states = dot_tn(heads[:, cols], c_ref[...])
        for piece in range(8):
            local_ref[8 * part + piece] = states[48 * piece : 48 * piece + 48].astype(bf16)


def gate_back(grad, weight, y, proj, pre, vbc, cum, gain, skip):
    whole = lambda k: (0, 0)
    return call(
        gate_back_kernel,
        (
            sds((ROWS, D), bf16),
            sds((ROWS, INNER), bf16),
            sds((ROWS, INNER), bf16),
            sds((32, 48, LANES), bf16),
            sds((ROWS, LANES), f32),
            sds((1, INNER), f32),
            sds((8, LANES), f32),
        ),
        scratch=[
            pltpu.VMEM((ROWS, INNER), f32),
            pltpu.VMEM((ROWS, INNER), f32),
            pltpu.VMEM((ROWS, INNER), bf16),
            pltpu.VMEM((ROWS, INNER), bf16),
            pltpu.VMEM((ROWS, INNER), bf16),
        ],
        grid=(1,),
        in_specs=[
            pl.BlockSpec((ROWS, D), whole),
            pl.BlockSpec((INNER, D), whole),
            pl.BlockSpec((ROWS, INNER), whole),
            pl.BlockSpec((ROWS, INNER), whole),
            pl.BlockSpec((ROWS, INNER), whole),
            pl.BlockSpec((ROWS, LANES), lambda k: (0, 13)),
            pl.BlockSpec((ROWS, LANES), whole),
            pl.BlockSpec((1, INNER), whole),
            pl.BlockSpec((1, INNER), whole),
        ],
        out_specs=[
            pl.BlockSpec((ROWS, D), whole),
            pl.BlockSpec((ROWS, INNER), whole),
            pl.BlockSpec((ROWS, INNER), whole),
            pl.BlockSpec((32, 48, LANES), lambda k: (0, 0, 0)),
            pl.BlockSpec((ROWS, LANES), whole),
            pl.BlockSpec((1, INNER), whole),
            pl.BlockSpec((8, LANES), whole),
        ],
        flops=2 * ROWS * INNER * (D + LANES),
        moved=12_000_000,
        name="gate_back",
    )(grad, weight, y, proj, pre, vbc, cum, gain, skip)


def early_grads_kernel(core_ref, normed_ref, dz_ref, gated_ref, low_ref, keep_ref, send_ref):
    core = core_ref[0]
    normed_t = jnp.transpose(normed_ref[...])
    gated_t = jnp.transpose(gated_ref[...])
    for out_ref, side in ((keep_ref, core), (send_ref, 1 - core)):
        for k in range(2):
            col = pl.multiple_of((2 * k + side) * 384, LANES)
            total = dot(normed_t, dz_ref[:, pl.ds(col, 384)])
            for w in range(4):
                for rb in range(4):
                    row = 192 * w + 48 * rb
                    out_ref[4 * rb + k, w] = total[row : row + 48].astype(bf16)
        col = pl.multiple_of(side * 384, LANES)
        total = dot(gated_t, low_ref[:, pl.ds(col, 384)])
        for k in range(2):
            for w in range(4):
                for rb in range(4):
                    row = 384 * w + 192 * k + 48 * rb
                    out_ref[4 * rb + 2 + k, w] = total[row : row + 48].astype(bf16)


def early_grads(core, normed, dz, gated, low):
    shape = sds((16, 4, 48, 384), bf16)
    whole = pl.BlockSpec(memory_space=pltpu.VMEM)
    return call(
        early_grads_kernel,
        (shape, shape),
        in_specs=[pl.BlockSpec(memory_space=pltpu.SMEM)] + [whole] * 4,
        out_specs=[whole] * 2,
        flops=4 * ROWS * INNER * D,
        moved=7_000_000,
        name="early_grads",
    )(core, normed, dz, gated, low)


def within_back_kernel(vbc_ref, dy_ref, cum_ref, state_ref, dv_ref, dbc_ref, score, pile):
    b_part = vbc_ref[:, INNER : INNER + NSTATE]
    c_part = vbc_ref[:, INNER + NSTATE :]
    keep = iota((ROWS, ROWS), 0) <= iota((ROWS, ROWS), 1)
    score[...] = jnp.where(keep, dot_nt(b_part, c_part), 0.0)
    pile[...] = jnp.zeros_like(pile)
    cum = cum_ref[...]
    cum_t = jnp.transpose(cum)
    grown = jnp.exp(cum)
    left = iota((LANES, LANES), 1) < HDIM
    left_all = iota((ROWS, LANES), 1) < HDIM
    dc = jnp.zeros((ROWS, NSTATE), f32)
    for p in range(PAIRS):
        cols = slice(p * LANES, (p + 1) * LANES)
        values, dy = vbc_ref[:, cols], dy_ref[:, cols]
        tops, lows = [], []
        for side, h in enumerate((2 * p, 2 * p + 1)):
            col, row = cum[:, h : h + 1], cum_t[h : h + 1, :]
            mine = left_all if side == 0 else jnp.logical_not(left_all)
            own = jnp.where(mine, values.astype(f32), 0.0).astype(bf16)
            top = jnp.exp(jnp.minimum(row - col[0:LANES], 0.0))
            low = jnp.exp(jnp.minimum(row[:, LANES:] - col[LANES:], 0.0))
            tops.append(dot((top * score[0:LANES, :]).astype(bf16), dy))
            lows.append(dot((low * score[LANES:, LANES:]).astype(bf16), dy[LANES:]))
            pile[0:LANES, :] += top * dot_nt(own[0:LANES], dy)
            pile[LANES:, LANES:] += low * dot_nt(own[LANES:], dy[LANES:])
        dv_ref[0:LANES, cols] = jnp.where(left, tops[0], tops[1])
        dv_ref[LANES:, cols] = jnp.where(left, lows[0], lows[1])
        lifted = (dy.astype(f32) * pair_of(grown, p)).astype(bf16)
        dc = dc + dot(lifted, state_ref[cols, :])
    dscore = jnp.where(keep, pile[...], 0.0).astype(bf16)
    dbc_ref[:, 0:NSTATE] = dot(dscore, c_part)
    dbc_ref[:, NSTATE:] = dc + dot_tn(dscore, b_part)


def within_back(vbc, dy, cum, states):
    return call(
        within_back_kernel,
        (sds((ROWS, INNER), f32), sds((ROWS, 2 * NSTATE), f32)),
        scratch=[pltpu.VMEM((ROWS, ROWS), f32), pltpu.VMEM((ROWS, ROWS), f32)],
        flops=2 * HEADS * ROWS * ROWS * LANES * 6,
        moved=4_000_000,
        name="within_back",
    )(vbc, dy, cum, states)


def conv_back_kernel(
    later_ref, state_ref, dv_ref, dy_ref, vbc_ref, pre_ref, proj_ref, edge_ref, taps_ref, skip_ref,
    b_ref, cum_ref, step_ref, dt_ref, dbc_ref, row_ref, decay_ref, dtb_ref,
    pg_ref, edge_grad_ref, param_ref, ddt_ref, vec_ref,
    ext_in, ext_out, tail_keep, acc_b, acc_v, acc_x, acc_t, acc_s,
):
    k = pl.program_id(0)

    @pl.when(k == 0)
    def _():
        cum = cum_ref[...]
        tail_keep[...] = jnp.exp(cum[ROWS - 1 : ROWS] - cum)
        acc_b[...] = jnp.zeros_like(acc_b)
        acc_v[...] = jnp.zeros_like(acc_v)
        acc_x[...] = jnp.zeros_like(acc_x)
        acc_t[...] = jnp.zeros_like(acc_t)
        acc_s[...] = jnp.zeros_like(acc_s)
        ext_out[0:8] = jnp.zeros((8, 256), f32)
        ext_out[ROWS + 8 :] = jnp.zeros((8, 256), f32)

    pre = pre_ref[...]
    sig = sigmoid(pre)

    @pl.when(k < 6)
    def _():
        mask = head_mask(256, 4 * k)
        high, low = split2(step_ref[...])
        step = dot_nt(high, mask) + dot_nt(low, mask)
        high, low = split2(tail_keep[...])
        tail = dot_nt(high, mask) + dot_nt(low, mask)
        later = later_ref[...]
        value = vbc_ref[...].astype(f32)
        acc_b[...] += dot((value * tail).astype(bf16), later)
        from_state = tail * dot_nt(b_ref[...], later)
        dv = dv_ref[...] + from_state
        x = pre * sig
        high, low = split2(value * dv)
        acc_v[...] += dot(high, mask) + dot(low, mask)
        high, low = split2(x * dv)
        acc_x[...] += dot(high, mask) + dot(low, mask)
        sums = jnp.broadcast_to(jnp.sum(value * from_state, axis=0, keepdims=True), (16, 256))
        high, low = split2(sums)
        acc_t[...] += (dot(high, mask) + dot(low, mask))[0:8]
        high, low = split2(later.astype(f32) * state_ref[...].astype(f32))
        ones = jnp.ones((16, NSTATE), bf16)
        high, low = split2(dot_nt(ones, high) + dot_nt(ones, low))
        acc_s[...] += (dot(high, mask) + dot(low, mask))[0:8]
        ext_out[8 : 8 + ROWS] = step * dv + skip_ref[...] * dy_ref[...].astype(f32)

    @pl.when(k == 6)
    def _():
        ext_out[8 : 8 + ROWS, 0:NSTATE] = dbc_ref[:, 0:NSTATE] + acc_b[...]
        ext_out[8 : 8 + ROWS, NSTATE:] = dbc_ref[:, NSTATE:]
        inside = iota((ROWS, LANES), 1) < HEADS
        raw = jnp.where(inside, dt_ref[...], 0.0) + dtb_ref[...]
        rate = jnp.exp(decay_ref[...])
        log_decay = -step_ref[...] * rate
        whole = acc_t[0:1] + jnp.exp(cum_ref[ROWS - 1 : ROWS]) * acc_s[0:1]
        dlog = running_sum(row_ref[...] - acc_v[...], True) + whole
        dstep = acc_x[...] - dlog * rate
        ddt = jnp.where(inside, dstep * sigmoid(raw), 0.0)
        ddt_ref[...] = ddt.astype(bf16)
        vec_ref[0:1] = jnp.sum(jnp.where(inside, dlog * log_decay, 0.0), axis=0, keepdims=True)
        vec_ref[1:2] = jnp.sum(ddt, axis=0, keepdims=True)
        vec_ref[2:8] = jnp.zeros((6, LANES), f32)

    ds = ext_out[8 : 8 + ROWS] * (sig * (1.0 + pre * (1.0 - sig)))
    ext_out[8 : 8 + ROWS] = ds
    ext_in[0:8] = edge_ref[...]
    ext_in[8 : 8 + ROWS] = proj_ref[...]
    grad = taps_ref[3:4] * ds
    edge_grad = taps_ref[3:4] * ext_out[0:8]
    param_ref[3:4] = jnp.sum(ds * ext_in[8 : 8 + ROWS], axis=0, keepdims=True)
    for tap in range(WIDTH - 1):
        ahead = WIDTH - 1 - tap
        weight = taps_ref[tap : tap + 1]
        grad = grad + weight * ext_out[8 + ahead : 8 + ahead + ROWS]
        edge_grad = edge_grad + weight * ext_out[ahead : ahead + 8]
        param_ref[tap : tap + 1] = jnp.sum(ds * ext_in[5 + tap : 5 + tap + ROWS], axis=0, keepdims=True)
    param_ref[4:5] = jnp.sum(ds, axis=0, keepdims=True)
    param_ref[5:8] = jnp.zeros((3, 256), f32)
    pg_ref[...] = grad
    edge_grad_ref[...] = edge_grad


def conv_back(later, states, dv, dy, vbc, pre, proj, edge, taps, skip, cum, step, dbc, row, decay, dtb):
    block = 256
    upto = lambda k: jnp.minimum(k, 5)
    whole = lambda k: (0, 0)
    return call(
        conv_back_kernel,
        (
            sds((ROWS, CONV), f32),
            sds((8, CONV), f32),
            sds((8, CONV), f32),
            sds((ROWS, LANES), bf16),
            sds((8, LANES), f32),
        ),
        scratch=[
            pltpu.VMEM((ROWS + 8, block), f32),
            pltpu.VMEM((ROWS + 16, block), f32),
            pltpu.VMEM((ROWS, LANES), f32),
            pltpu.VMEM((ROWS, NSTATE), f32),
            pltpu.VMEM((ROWS, LANES), f32),
            pltpu.VMEM((ROWS, LANES), f32),
            pltpu.VMEM((8, LANES), f32),
            pltpu.VMEM((8, LANES), f32),
        ],
        grid=(7,),
        in_specs=[
            pl.BlockSpec((block, NSTATE), lambda k: (upto(k), 0)),
            pl.BlockSpec((block, NSTATE), lambda k: (upto(k), 0)),
            pl.BlockSpec((ROWS, block), lambda k: (0, upto(k))),
            pl.BlockSpec((ROWS, block), lambda k: (0, upto(k))),
            pl.BlockSpec((ROWS, block), lambda k: (0, k)),
            pl.BlockSpec((ROWS, block), lambda k: (0, k)),
            pl.BlockSpec((ROWS, block), lambda k: (0, 6 + k)),
            pl.BlockSpec((8, block), lambda k: (0, k)),
            pl.BlockSpec((WIDTH, block), lambda k: (0, k)),
            pl.BlockSpec((1, block), lambda k: (0, upto(k))),
            pl.BlockSpec((ROWS, NSTATE), lambda k: (0, 12)),
            pl.BlockSpec((ROWS, LANES), whole),
            pl.BlockSpec((ROWS, LANES), whole),
            pl.BlockSpec((ROWS, LANES), lambda k: (0, 26)),
            pl.BlockSpec((ROWS, 2 * NSTATE), whole),
            pl.BlockSpec((ROWS, LANES), whole),
            pl.BlockSpec((1, LANES), whole),
            pl.BlockSpec((1, LANES), whole),
        ],
        out_specs=[
            pl.BlockSpec((ROWS, block), lambda k: (0, k)),
            pl.BlockSpec((8, block), lambda k: (0, k)),
            pl.BlockSpec((8, block), lambda k: (0, k)),
            pl.BlockSpec((ROWS, LANES), whole),
            pl.BlockSpec((8, LANES), whole),
        ],
        flops=6 * ROWS * INNER * NSTATE,
        moved=12_000_000,
        name="conv_back",
    )(
        later, states, dv, dy, vbc, pre, proj, edge, taps, skip,
        vbc, cum, step, proj, dbc, row, decay, dtb,
    )


def norm_back_kernel(
    pg_ref, next_ref, dz_ref, ddt_ref, w_ref, x_ref, gain_ref, grad_ref,
    low_ref, out_ref, dgain_ref,
):
    low_ref[0 : ROWS - 16] = pg_ref[0 : ROWS - 16].astype(bf16)
    last = pg_ref[ROWS - 16 :]
    low_ref[ROWS - 16 :] = jnp.concatenate([last[0:8], last[8:16] + next_ref[...]]).astype(bf16)
    back = dot_nt(dz_ref[...], w_ref[:, 0:INNER])
    back = back + dot_nt(low_ref[...], w_ref[:, INNER : INNER + CONV])
    back = back + dot_nt(ddt_ref[:, 0:HEADS], w_ref[:, INNER + CONV : PROJ])
    x = x_ref[...].astype(f32)
    scale = lax.rsqrt(jnp.mean(x * x, axis=-1, keepdims=True) + EPS)
    dgain_ref[...] = jnp.sum(back * x * scale, axis=0, keepdims=True)
    scaled = back * gain_ref[...]
    pull = scale * scale * scale * jnp.mean(scaled * x, axis=-1, keepdims=True)
    out_ref[...] = grad_ref[...].astype(f32) + scaled * scale - x * pull


def norm_back(pg, following, dz, ddt, weight, x, gain, grad):
    return call(
        norm_back_kernel,
        (sds((ROWS, CONV), bf16), sds((ROWS, D), f32), sds((1, D), f32)),
        flops=2 * ROWS * D * PROJ,
        moved=11_000_000,
        name="norm_back",
    )(pg, following, dz, ddt, weight, x, gain, grad)


def late_grads_kernel(
    core_ref, normed_ref, low_ref, ddt_ref, dgain_in_ref, dgain_out_ref, param_ref, vec_ref, dskip_ref,
    keep_ref, send_ref, small,
):
    core = core_ref[0]
    small[...] = jnp.zeros_like(small)
    line = 0
    for ref, first, count in ((dgain_in_ref, 0, 6), (dgain_out_ref, 0, 12)):
        for i in range(count):
            small[line : line + 1, :] = ref[first : first + 1, LANES * i : LANES * i + LANES]
            line += 1
    for tap in range(WIDTH + 1):
        for i in range(CONV // LANES):
            small[line : line + 1, :] = param_ref[tap : tap + 1, LANES * i : LANES * i + LANES]
            line += 1
    vec = vec_ref[...]
    lane = iota((8, LANES), 1)
    decay = jnp.where(lane < HEADS, jnp.broadcast_to(vec[0:1], (8, LANES)), 0.0)
    dtb = jnp.where(lane < HEADS, jnp.broadcast_to(vec[1:2], (8, LANES)), 0.0)
    skip = jnp.where(lane < HEADS, dskip_ref[...], 0.0)
    joined = decay + pltpu.roll(dtb, HEADS, 1) + pltpu.roll(skip, 2 * HEADS, 1)
    small[line : line + 1, :] = joined[0:1]

    normed_t = jnp.transpose(normed_ref[...])

    def place(out_ref, k, lanes, total):
        for w in range(4):
            for rb in range(4):
                row = 192 * w + 48 * rb
                out_ref[4 * rb + k, w, :, lanes] = total[row : row + 48].astype(bf16)

    for out_ref, side in ((keep_ref, core), (send_ref, 1 - core)):
        for k in range(3):
            col = pl.multiple_of((2 * k + side) * 256, LANES)
            place(out_ref, k, slice(0, 256), dot(normed_t, low_ref[:, pl.ds(col, 256)]))

        @pl.when(side == 0)
        def _(out_ref=out_ref):
            place(out_ref, 3, slice(0, 256), dot(normed_t, low_ref[:, 1536:1792]))

        @pl.when(side == 1)
        def _(out_ref=out_ref):
            place(out_ref, 3, slice(0, 128), dot(normed_t, ddt_ref[...]))
            for w in range(4):
                for rb in range(4):
                    if rb < 2:
                        block = small[48 * rb : 48 * rb + 48, :]
                    else:
                        block = jnp.zeros((48, LANES), f32)
                    out_ref[4 * rb + 3, w, :, 128:256] = block.astype(bf16)


def late_grads(core, normed, low, ddt, dgain_in, dgain_out, param, vec, dskip):
    shape = sds((16, 4, 48, 256), bf16)
    whole = pl.BlockSpec(memory_space=pltpu.VMEM)
    return call(
        late_grads_kernel,
        (shape, shape),
        scratch=[pltpu.VMEM((96, LANES), f32)],
        in_specs=[pl.BlockSpec(memory_space=pltpu.SMEM)] + [whole] * 8,
        out_specs=[whole] * 2,
        flops=2 * ROWS * D * CONV,
        moved=5_000_000,
        name="late_grads",
    )(core, normed, low, ddt, dgain_in, dgain_out, param, vec, dskip)


def adam_step(weight, moment, second, gradient, learn_rate, weight_decay):
    new_moment = 0.9 * moment + 0.1 * gradient
    new_second = 0.95 * second + 0.05 * gradient * gradient
    corrected = new_moment / (1.0 - 0.9**STEP) / (jnp.sqrt(new_second / (1.0 - 0.95**STEP)) + 1e-08)
    return (new_moment, new_second, weight - learn_rate * (corrected + weight_decay * weight))


def adam_in_kernel(zo_ref, cs_ref, w_ref, m_ref, v_ref, *refs):
    m_out, v_out, w_out = refs[-3:]

    def update(first, width, grad):
        cols = slice(first, first + width)
        new_m, new_v, new_w = adam_step(
            w_ref[0, :, cols], m_ref[0, :, cols], v_ref[0, :, cols], grad.astype(f32), 0.03, 0.1
        )
        m_out[0, :, cols] = new_m
        v_out[0, :, cols] = new_v
        w_out[0, :, cols] = new_w

    for cb in range(4):
        update(384 * cb, 384, zo_ref[0, cb])
    for cb in range(7):
        update(INNER + 256 * cb, 256, cs_ref[0, cb])
    update(INNER + CONV, HEADS, cs_ref[0, 7][:, 0:HEADS])


def adam_in(zo, cs, w, m, v, layer, before):
    state = pl.BlockSpec((1, 48, PROJ), lambda r: (layer, r, 0))
    shape = sds((2, 192, PROJ), f32)
    aliases = {} if before is None else {5: 0, 6: 1, 7: 2}
    held = () if before is None else tuple(before)
    return call(
        adam_in_kernel,
        (shape, shape, shape),
        grid=(4,),
        in_specs=[
            pl.BlockSpec((1, 8, 48, 384), lambda r: (r, 0, 0, 0)),
            pl.BlockSpec((1, 8, 48, 256), lambda r: (r, 0, 0, 0)),
            state,
            state,
            state,
        ]
        + [pl.BlockSpec(memory_space=pl.ANY)] * len(held),
        out_specs=[state] * 3,
        input_output_aliases=aliases,
        moved=17_000_000,
        name="adam_in",
    )(zo, cs, w, m, v, *held)


def adam_out_kernel(zo_ref, w_ref, m_ref, v_ref, *refs):
    m_out, v_out, w_out = refs[-3:]
    for half in range(2):
        for cb in range(2):
            cols = slice(384 * cb, 384 * cb + 384)
            new_m, new_v, new_w = adam_step(
                w_ref[0, half, :, cols], m_ref[0, half, :, cols], v_ref[0, half, :, cols],
                zo_ref[0, 4 + 2 * half + cb].astype(f32), 0.02, 0.1,
            )
            m_out[0, half, :, cols] = new_m
            v_out[0, half, :, cols] = new_v
            w_out[0, half, :, cols] = new_w


def adam_out(zo, w, m, v, layer, before):
    state = pl.BlockSpec((1, 2, 48, D), lambda r: (layer, 0, r, 0))
    shape = sds((2, 2, 192, D), f32)
    aliases = {} if before is None else {4: 0, 5: 1, 6: 2}
    held = () if before is None else tuple(before)
    return call(
        adam_out_kernel,
        (shape, shape, shape),
        grid=(4,),
        in_specs=[
            pl.BlockSpec((1, 8, 48, 384), lambda r: (r, 0, 0, 0)),
            state,
            state,
            state,
        ]
        + [pl.BlockSpec(memory_space=pl.ANY)] * len(held),
        out_specs=[state] * 3,
        input_output_aliases=aliases,
        moved=8_000_000,
        name="adam_out",
    )(zo, w, m, v, *held)


def next_in_sequence(rows, step):
    route = [(i, i + step) for i in range(32) if 0 <= i + step < 32]
    return lax.ppermute(rows, PLANE, route)


def exchange(blocks):
    return lax.all_to_all(blocks, PLANE, 0, 0, tiled=True)


def reduce_pieces(keep, send):
    received = lax.ppermute(send, "core", [(0, 1), (1, 0)])
    paired = (keep.astype(f32) + received.astype(f32)).astype(bf16)
    width = keep.shape[-1]
    parts = lax.all_to_all(paired.reshape(64, 48, width), ("x", "z", "wt"), 0, 0, tiled=True)
    total = jnp.sum(parts.astype(f32), axis=0).astype(bf16)
    spread = exchange(jnp.broadcast_to(total[None], (32, 48, width)))
    return spread.reshape(4, 8, 48, width)


def shards(
    tokens, in_w, in_m, in_v, out_w, out_m, out_v, small_params, small_m, small_v, cotangent
):
    core = lax.axis_index("core").astype(jnp.int32).reshape(1)
    tokens = tokens[0]
    cotangent = cotangent[0]
    in_full, out_full = [], []
    for layer in range(2):
        in_full.append(lax.all_gather(in_w[layer].astype(bf16), "wt", axis=0, tiled=True))
        out_full.append(lax.all_gather(out_w[layer].astype(bf16), "wt", axis=0, tiled=True))
    small_full = lax.all_gather(small_params.astype(bf16), "wt", axis=1, tiled=True).astype(f32)

    def heads_row(first):
        return jnp.pad(small_full[:, first : first + HEADS], ((0, 0), (0, LANES - HEADS)))

    gain_in = small_full[:, :D]
    gain_out = small_full[:, D : D + INNER]
    taps = small_full[:, 2304:9472].reshape(2, WIDTH, CONV)
    bias = small_full[:, 9472:11264]
    decay = heads_row(11264)
    dtb = heads_row(11264 + HEADS)
    skip = jnp.repeat(small_full[:, 11264 + 2 * HEADS : VEC], HDIM, axis=1)

    hidden = tokens
    saved = []
    for layer in range(2):
        row = slice(layer, layer + 1)
        edge = next_in_sequence(hidden[ROWS - 8 :], 1)
        normed, proj = project(hidden, gain_in[row], in_full[layer])
        pre, edge_in, vbc, cum, step, pay = conv_states(
            edge, gain_in[row], in_full[layer], proj, taps[layer], bias[row], decay[row], dtb[row]
        )
        slices = exchange(pay)
        yw = within(vbc, cum)
        scanned, chain = scan_states(slices)
        states = exchange(scanned).reshape(INNER, NSTATE)
        after, y, gated = output_part(
            yw, vbc, cum, pre, proj, states, hidden, out_full[layer], gain_out[row], skip[row]
        )
        saved.append((hidden, normed, proj, pre, edge_in, vbc, cum, step, chain, states, y, gated))
        hidden = after

    grad = cotangent
    reduced = [None, None]
    for layer in (1, 0):
        row = slice(layer, layer + 1)
        start, normed, proj, pre, edge_in, vbc, cum, step, chain, states, y, gated = saved[layer]
        low, dz, dy, local, rows_sum, dgain_out, dskip = gate_back(
            grad, out_full[layer], y, proj, pre, vbc, cum, gain_out[row], skip[row]
        )
        slices = exchange(local)
        dv, dbc = within_back(vbc, dy, cum, states)
        early = early_grads(core, normed, dz, gated, low)
        later = exchange(scan_back(slices, chain)).reshape(INNER, NSTATE)
        pg, edge_grad, param, ddt, vec = conv_back(
            later, states, dv, dy, vbc, pre, proj, edge_in, taps[layer], skip[row],
            cum, step, dbc, rows_sum, decay[row], dtb[row],
        )
        following = next_in_sequence(edge_grad, -1)
        pg_low, grad, dgain_in = norm_back(
            pg, following, dz, ddt, in_full[layer], start, gain_in[row], grad
        )
        late = late_grads(core, normed, pg_low, ddt, dgain_in, dgain_out, param, vec, dskip)
        reduced[layer] = (reduce_pieces(*early), reduce_pieces(*late))

    split = lambda a: a.reshape(2, 2, 192, D)
    new_in, new_out = None, None
    for layer in (1, 0):
        zo, cs = reduced[layer]
        new_in = adam_in(zo, cs, in_w, in_m, in_v, layer, new_in)
        new_out = adam_out(zo, split(out_w), split(out_m), split(out_v), layer, new_out)
    small_total = jnp.stack([cs[0:2, 7, :, 128:256].reshape(96 * LANES)[:VEC] for _, cs in reduced])
    width = VEC // 4
    small_total = lax.dynamic_slice_in_dim(
        small_total.astype(f32), lax.axis_index("wt") * width, width, 1
    )
    new_small = adam_step(small_params, small_m, small_v, small_total, 0.2, 0.0)
    return (
        hidden[None],
        grad[None],
        *new_in,
        *(a.reshape(2, 384, D) for a in new_out),
        *new_small,
    )


def solution(mesh):
    fine = Mesh(mesh.devices.reshape(4, 4, 2, 4), ("x", "z", "core", "wt"))
    rows = P("wt", PLANE, None)
    held = P(None, "wt", None)
    flat = P(None, "wt")
    return jax.shard_map(
        shards,
        mesh=fine,
        in_specs=(rows, held, held, held, held, held, held, flat, flat, flat, rows),
        out_specs=(rows, rows, held, held, held, held, held, held, flat, flat, flat),
        check_vma=False,
    )
```

```python
import functools

import jax
import jax.numpy as jnp
from jax import lax
from jax.experimental import pallas as pl
from jax.experimental.pallas import tpu as pltpu
from jax.sharding import Mesh
from jax.sharding import PartitionSpec as P

D = 768
HEADS = 24
HDIM = 64
NSTATE = 128
WIDTH = 4
STEP = 10
INNER = 1536
CONV = 1792
PROJ = 3352
VEC = 11336
ROWS = 256
EPS = 1e-05
PAIRS = HEADS // 2
LANES = 128
PLANE = ("x", "z", "core")

bf16 = jnp.bfloat16
f32 = jnp.float32
MIB = 1024 * 1024


def call(kernel, outs, scratch=(), grid=(), in_specs=None, out_specs=None, flops=0, moved=0, vmem=60, **kw):
    params = pltpu.CompilerParams(vmem_limit_bytes=vmem * MIB)
    extra = {}
    if in_specs is not None:
        extra["in_specs"] = in_specs
        extra["out_specs"] = out_specs
    return pl.pallas_call(
        kernel,
        out_shape=outs,
        grid=grid,
        scratch_shapes=list(scratch),
        compiler_params=params,
        cost_estimate=pl.CostEstimate(flops=flops, bytes_accessed=moved, transcendentals=0),
        **extra,
        **kw,
    )


def sds(shape, dtype):
    return jax.ShapeDtypeStruct(shape, dtype)


def dot(a, b):
    return lax.dot_general(a, b, (((1,), (0,)), ((), ())), preferred_element_type=f32)


def dot_nt(a, b):
    return lax.dot_general(a, b, (((1,), (1,)), ((), ())), preferred_element_type=f32)


def dot_tn(a, b):
    return lax.dot_general(a, b, (((0,), (0,)), ((), ())), preferred_element_type=f32)


def split2(v):
    high = v.astype(bf16)
    return high, (v - high.astype(f32)).astype(bf16)


def split3(v):
    high = v.astype(bf16)
    rest = v - high.astype(f32)
    mid = rest.astype(bf16)
    return high, mid, (rest - mid.astype(f32)).astype(bf16)


def iota(shape, dim):
    return lax.broadcasted_iota(jnp.int32, shape, dim)


def sigmoid(v):
    return 1.0 / (1.0 + jnp.exp(-v))


def softplus(v):
    return jnp.maximum(v, 0.0) + jnp.log1p(jnp.exp(-jnp.abs(v)))


def pair_of(v, p):
    rows = v.shape[0]
    left = jnp.broadcast_to(v[:, 2 * p : 2 * p + 1], (rows, LANES))
    right = jnp.broadcast_to(v[:, 2 * p + 1 : 2 * p + 2], (rows, LANES))
    return jnp.where(iota((rows, LANES), 1) < HDIM, left, right)


def head_mask(columns, first_head):
    return ((iota((columns, LANES), 0) >> 6) + first_head == iota((columns, LANES), 1)).astype(bf16)


def running_sum(v, reverse):
    rows, cols = iota((ROWS, ROWS), 0), iota((ROWS, ROWS), 1)
    tri = ((cols >= rows) if reverse else (cols <= rows)).astype(bf16)
    high, mid, low = split3(v)
    return dot(tri, high) + dot(tri, mid) + dot(tri, low)


def project_kernel(x_ref, gain_ref, w_ref, normed_ref, proj_ref):
    @pl.when(pl.program_id(0) == 0)
    def _():
        x = x_ref[...].astype(f32)
        scale = lax.rsqrt(jnp.mean(x * x, axis=-1, keepdims=True) + EPS)
        normed_ref[...] = (x * scale * gain_ref[...]).astype(bf16)

    proj_ref[...] = dot(normed_ref[...], w_ref[...])


def project(x, gain, weight):
    block = 512
    return call(
        project_kernel,
        (sds((ROWS, D), bf16), sds((ROWS, PROJ), f32)),
        grid=(pl.cdiv(PROJ, block),),
        in_specs=[
            pl.BlockSpec((ROWS, D), lambda k: (0, 0)),
            pl.BlockSpec((1, D), lambda k: (0, 0)),
            pl.BlockSpec((D, block), lambda k: (0, k)),
        ],
        out_specs=[
            pl.BlockSpec((ROWS, D), lambda k: (0, 0)),
            pl.BlockSpec((ROWS, block), lambda k: (0, k)),
        ],
        flops=2 * ROWS * D * PROJ,
        moved=9_500_000,
        name="project",
    )(x, gain, weight)


def conv_kernel(
    edge_ref, gain_ref, w_ref, proj_ref, dt_ref, taps_ref, bias_ref, decay_ref, dtb_ref,
    pre_ref, edge_out_ref, vbc_ref, cum_ref, step_ref, pay_ref,
    edge_n, ext, b_keep, tail_keep, states,
):
    k = pl.program_id(0)

    @pl.when(k == 0)
    def _():
        edge = edge_ref[...].astype(f32)
        scale = lax.rsqrt(jnp.mean(edge * edge, axis=-1, keepdims=True) + EPS)
        edge_n[0:8] = edge * scale * gain_ref[...]
        edge_n[8:16] = jnp.zeros((8, D), f32)
        inside = iota((ROWS, LANES), 1) < HEADS
        raw = jnp.where(inside, dt_ref[...], 0.0)
        step = jnp.where(inside, softplus(raw + dtb_ref[...]), 0.0)
        cum = running_sum(-step * jnp.exp(decay_ref[...]), False)
        step_ref[...] = step
        cum_ref[...] = cum
        tail_keep[...] = jnp.exp(cum[ROWS - 1 : ROWS] - cum)

    edge_in = dot(edge_n[...].astype(bf16), w_ref[...])[0:8]
    edge_out_ref[...] = edge_in
    ext[0:8] = edge_in
    ext[8 : 8 + ROWS] = proj_ref[...]
    total = bias_ref[...] + taps_ref[0:1] * ext[5 : 5 + ROWS]
    for tap in range(1, WIDTH):
        total = total + taps_ref[tap : tap + 1] * ext[5 + tap : 5 + tap + ROWS]
    pre_ref[...] = total
    out = total * sigmoid(total)

    @pl.when(k == 0)
    def _():
        vbc_ref[...] = out.astype(bf16)
        b_keep[...] = out[:, :NSTATE].astype(bf16)

    @pl.when(k > 0)
    def _():
        mask = head_mask(256, 4 * (k - 1))
        s_high, s_low = split2(step_ref[...])
        value = out * (dot_nt(s_high, mask) + dot_nt(s_low, mask))
        vbc_ref[...] = value.astype(bf16)
        t_high, t_low = split2(tail_keep[...])
        tailed = value * (dot_nt(t_high, mask) + dot_nt(t_low, mask))
        row = pl.multiple_of((k - 1) * 256, 256)
        states[pl.ds(row, 256), :] = dot_tn(tailed.astype(bf16), b_keep[...])

    @pl.when(k == 6)
    def _():
        total_log = cum_ref[ROWS - 1 : ROWS, :]
        piece = iota((32, LANES), 0)
        head = (piece * 48 + iota((32, LANES), 1)) >> 6
        logs = jnp.zeros((32, LANES), f32)
        for h in range(HEADS):
            logs = jnp.where(head == h, total_log[:, h : h + 1], logs)
        row16 = iota((16, LANES), 0)
        for piece in range(32):
            pay_ref[piece, 0:48, :] = states[48 * piece : 48 * piece + 48, :].astype(bf16)
            line = logs[piece : piece + 1, :]
            high = line.astype(bf16).astype(f32)
            extra = jnp.where(row16 == 0, high, jnp.where(row16 == 1, line - high, 0.0))
            pay_ref[piece, 48:64, :] = extra.astype(bf16)


def conv_states(edge, gain, weight, proj, taps, bias, decay, dtb):
    block = 256
    turn = lambda k: (k + 6) % 7
    whole = lambda k: (0, 0)
    return call(
        conv_kernel,
        (
            sds((ROWS, CONV), f32),
            sds((8, CONV), f32),
            sds((ROWS, CONV), bf16),
            sds((ROWS, LANES), f32),
            sds((ROWS, LANES), f32),
            sds((32, 64, LANES), bf16),
        ),
        scratch=[
            pltpu.VMEM((16, D), f32),
            pltpu.VMEM((ROWS + 8, block), f32),
            pltpu.VMEM((ROWS, NSTATE), bf16),
            pltpu.VMEM((ROWS, LANES), f32),
            pltpu.VMEM((INNER, NSTATE), f32),
        ],
        grid=(7,),
        in_specs=[
            pl.BlockSpec((8, D), whole),
            pl.BlockSpec((1, D), whole),
            pl.BlockSpec((D, block), lambda k: (0, 6 + turn(k))),
            pl.BlockSpec((ROWS, block), lambda k: (0, 6 + turn(k))),
            pl.BlockSpec((ROWS, LANES), lambda k: (0, 26)),
            pl.BlockSpec((WIDTH, block), lambda k: (0, turn(k))),
            pl.BlockSpec((1, block), lambda k: (0, turn(k))),
            pl.BlockSpec((1, LANES), whole),
            pl.BlockSpec((1, LANES), whole),
        ],
        out_specs=[
            pl.BlockSpec((ROWS, block), lambda k: (0, turn(k))),
            pl.BlockSpec((8, block), lambda k: (0, turn(k))),
            pl.BlockSpec((ROWS, block), lambda k: (0, turn(k))),
            pl.BlockSpec((ROWS, LANES), whole),
            pl.BlockSpec((ROWS, LANES), whole),
            pl.BlockSpec((32, 64, LANES), lambda k: (0, 0, 0)),
        ],
        flops=2 * ROWS * INNER * NSTATE + 2 * 16 * D * CONV,
        moved=9_000_000,
        name="conv_states",
    )(edge, gain, weight, proj, proj, taps, bias, decay, dtb)


def within_kernel(vbc_ref, cum_ref, y_ref, score):
    b_part = vbc_ref[:, INNER : INNER + NSTATE]
    c_part = vbc_ref[:, INNER + NSTATE :]
    keep = iota((ROWS, ROWS), 0) >= iota((ROWS, ROWS), 1)
    score[...] = jnp.where(keep, dot_nt(c_part, b_part), 0.0)
    cum = cum_ref[...]
    cum_t = jnp.transpose(cum)
    left = iota((LANES, LANES), 1) < HDIM
    for p in range(PAIRS):
        values = vbc_ref[:, p * LANES : (p + 1) * LANES]
        tops, lows = [], []
        for h in (2 * p, 2 * p + 1):
            col, row = cum[:, h : h + 1], cum_t[h : h + 1, :]
            top = jnp.exp(jnp.minimum(col[0:LANES] - row[:, 0:LANES], 0.0)) * score[0:LANES, 0:LANES]
            tops.append(dot(top.astype(bf16), values[0:LANES]))
            low = jnp.exp(jnp.minimum(col[LANES:] - row, 0.0)) * score[LANES:, :]
            lows.append(dot(low.astype(bf16), values))
        y_ref[0:LANES, p * LANES : (p + 1) * LANES] = jnp.where(left, tops[0], tops[1])
        y_ref[LANES:, p * LANES : (p + 1) * LANES] = jnp.where(left, lows[0], lows[1])


def within(vbc, cum):
    return call(
        within_kernel,
        sds((ROWS, INNER), f32),
        scratch=[pltpu.VMEM((ROWS, ROWS), f32)],
        flops=2 * HEADS * ROWS * ROWS * LANES * 4,
        moved=3_000_000,
        name="within",
    )(vbc, cum)


def scan_kernel(pay_ref, out_ref, decay_ref, logs):
    logs[...] = jnp.zeros_like(logs)
    for s in range(32):
        extra = pay_ref[s, 48:64, :].astype(f32)
        logs[s : s + 1, :] = extra[0:1] + extra[1:2]
    decay = jnp.exp(jnp.transpose(logs[...]))
    decay_ref[...] = decay
    carry = jnp.zeros((48, LANES), f32)
    for s in range(32):
        out_ref[s] = carry.astype(bf16)
        carry = decay[0:48, s : s + 1] * carry + pay_ref[s, 0:48, :].astype(f32)


def scan_states(pay):
    return call(
        scan_kernel,
        (sds((32, 48, LANES), bf16), sds((LANES, LANES), f32)),
        scratch=[pltpu.VMEM((LANES, LANES), f32)],
        moved=1_000_000,
        name="scan_states",
    )(pay)


def scan_back_kernel(grad_ref, decay_ref, out_ref):
    decay = decay_ref[...]
    carry = jnp.zeros((48, LANES), f32)
    for s in reversed(range(32)):
        out_ref[s] = carry.astype(bf16)
        carry = decay[0:48, s : s + 1] * carry + grad_ref[s].astype(f32)


def scan_back(grad, decay):
    return call(
        scan_back_kernel, sds((32, 48, LANES), bf16), moved=800_000, name="scan_back"
    )(grad, decay)


def output_kernel(
    yw_ref, c_ref, cum_ref, pre_ref, z_ref, state_ref, hid_ref, w_ref, gain_ref, skip_ref,
    hid_out, y_out, gated_ref, gate,
):
    grown = jnp.exp(cum_ref[...])
    c_part = c_ref[...]
    rows = hid_ref.shape[0]
    square = jnp.zeros((rows, 1), f32)
    for p in range(PAIRS):
        cols = slice(p * LANES, (p + 1) * LANES)
        y = yw_ref[:, cols] + dot_nt(c_part, state_ref[cols, :]) * pair_of(grown, p)
        y_out[:, cols] = y
        pre = pre_ref[:, cols]
        z = z_ref[:, cols]
        u = (y + skip_ref[:, cols] * (pre * sigmoid(pre))) * (z * sigmoid(z))
        gate[:, cols] = u
        square = square + jnp.sum(u * u, axis=-1, keepdims=True)
    scale = lax.rsqrt(square * (1.0 / INNER) + EPS)
    gated_ref[...] = (gate[...] * scale * gain_ref[...]).astype(bf16)
    hid_out[...] = hid_ref[...].astype(f32) + dot(gated_ref[...], w_ref[...])


def output_part(yw, vbc, cum, pre, proj, states, hidden, weight, gain, skip):
    rows = 128
    take = lambda k: (k, 0)
    whole = lambda k: (0, 0)
    return call(
        output_kernel,
        (sds((ROWS, D), f32), sds((ROWS, INNER), f32), sds((ROWS, INNER), bf16)),
        scratch=[pltpu.VMEM((rows, INNER), f32)],
        grid=(ROWS // rows,),
        in_specs=[
            pl.BlockSpec((rows, INNER), take),
            pl.BlockSpec((rows, LANES), lambda k: (k, 13)),
            pl.BlockSpec((rows, LANES), take),
            pl.BlockSpec((rows, INNER), take),
            pl.BlockSpec((rows, INNER), take),
            pl.BlockSpec((INNER, LANES), whole),
            pl.BlockSpec((rows, D), take),
            pl.BlockSpec((INNER, D), whole),
            pl.BlockSpec((1, INNER), whole),
            pl.BlockSpec((1, INNER), whole),
        ],
        out_specs=[
            pl.BlockSpec((rows, D), take),
            pl.BlockSpec((rows, INNER), take),
            pl.BlockSpec((rows, INNER), take),
        ],
        flops=2 * ROWS * INNER * (D + LANES),
        moved=10_000_000,
        name="output_part",
    )(yw, vbc, cum, pre, proj, states, hidden, weight, gain, skip)


def gate_back_kernel(
    grad_ref, w_ref, y_ref, z_ref, pre_ref, c_ref, cum_ref, gain_ref, skip_ref,
    low_ref, dz_ref, dy_ref, local_ref, row_ref, dgain_ref, dskip_ref,
    gate, back, high, low, heads,
):
    low_ref[...] = grad_ref[...].astype(bf16)
    back[...] = dot_nt(low_ref[...], w_ref[...])
    square = jnp.zeros((ROWS, 1), f32)
    cross = jnp.zeros((ROWS, 1), f32)
    for p in range(PAIRS):
        cols = slice(p * LANES, (p + 1) * LANES)
        pre, z = pre_ref[:, cols], z_ref[:, cols]
        u = (y_ref[:, cols] + skip_ref[:, cols] * (pre * sigmoid(pre))) * (z * sigmoid(z))
        gate[:, cols] = u
        square = square + jnp.sum(u * u, axis=-1, keepdims=True)
        cross = cross + jnp.sum(back[:, cols] * gain_ref[:, cols] * u, axis=-1, keepdims=True)
    scale = lax.rsqrt(square * (1.0 / INNER) + EPS)
    pull = scale * scale * scale * cross * (1.0 / INNER)
    grown = jnp.exp(cum_ref[...])
    for p in range(PAIRS):
        cols = slice(p * LANES, (p + 1) * LANES)
        pre, z, y = pre_ref[:, cols], z_ref[:, cols], y_ref[:, cols]
        u, grad = gate[:, cols], back[:, cols]
        x = pre * sigmoid(pre)
        dgain_ref[:, cols] = jnp.sum(grad * u * scale, axis=0, keepdims=True)
        du = grad * gain_ref[:, cols] * scale - u * pull
        sig = sigmoid(z)
        dssm = du * (z * sig)
        ssm = y + skip_ref[:, cols] * x
        dz_ref[:, cols] = (du * ssm * (sig * (1.0 + z * (1.0 - sig)))).astype(bf16)
        dy = dssm.astype(bf16)
        dy_ref[:, cols] = dy
        gate[0:1, cols] = jnp.sum(dssm * x, axis=0, keepdims=True)
        a, b = split2(dy.astype(f32) * y)
        high[:, cols] = a
        low[:, cols] = b
        heads[:, cols] = (dssm * pair_of(grown, p)).astype(bf16)
    mask = head_mask(INNER, 0)
    row_ref[...] = dot(high[...], mask) + dot(low[...], mask)
    a, b = split2(jnp.broadcast_to(gate[0:1, :], (16, INNER)))
    dskip_ref[...] = (dot(a, mask) + dot(b, mask))[0:8]
    for part in range(4):
        cols = slice(384 * part, 384 * part + 384)
        states = dot_tn(heads[:, cols], c_ref[...])
        for piece in range(8):
            local_ref[8 * part + piece] = states[48 * piece : 48 * piece + 48].astype(bf16)


def gate_back(grad, weight, y, proj, pre, vbc, cum, gain, skip):
    whole = lambda k: (0, 0)
    return call(
        gate_back_kernel,
        (
            sds((ROWS, D), bf16),
            sds((ROWS, INNER), bf16),
            sds((ROWS, INNER), bf16),
            sds((32, 48, LANES), bf16),
            sds((ROWS, LANES), f32),
            sds((1, INNER), f32),
            sds((8, LANES), f32),
        ),
        scratch=[
            pltpu.VMEM((ROWS, INNER), f32),
            pltpu.VMEM((ROWS, INNER), f32),
            pltpu.VMEM((ROWS, INNER), bf16),
            pltpu.VMEM((ROWS, INNER), bf16),
            pltpu.VMEM((ROWS, INNER), bf16),
        ],
        grid=(1,),
        in_specs=[
            pl.BlockSpec((ROWS, D), whole),
            pl.BlockSpec((INNER, D), whole),
            pl.BlockSpec((ROWS, INNER), whole),
            pl.BlockSpec((ROWS, INNER), whole),
            pl.BlockSpec((ROWS, INNER), whole),
            pl.BlockSpec((ROWS, LANES), lambda k: (0, 13)),
            pl.BlockSpec((ROWS, LANES), whole),
            pl.BlockSpec((1, INNER), whole),
            pl.BlockSpec((1, INNER), whole),
        ],
        out_specs=[
            pl.BlockSpec((ROWS, D), whole),
            pl.BlockSpec((ROWS, INNER), whole),
            pl.BlockSpec((ROWS, INNER), whole),
            pl.BlockSpec((32, 48, LANES), lambda k: (0, 0, 0)),
            pl.BlockSpec((ROWS, LANES), whole),
            pl.BlockSpec((1, INNER), whole),
            pl.BlockSpec((8, LANES), whole),
        ],
        flops=2 * ROWS * INNER * (D + LANES),
        moved=12_000_000,
        name="gate_back",
    )(grad, weight, y, proj, pre, vbc, cum, gain, skip)


def early_grads_kernel(core_ref, normed_ref, dz_ref, gated_ref, low_ref, keep_ref, send_ref):
    core = core_ref[0]
    normed_t = jnp.transpose(normed_ref[...])
    gated_t = jnp.transpose(gated_ref[...])
    for out_ref, side in ((keep_ref, core), (send_ref, 1 - core)):
        for k in range(2):
            col = pl.multiple_of((2 * k + side) * 384, LANES)
            total = dot(normed_t, dz_ref[:, pl.ds(col, 384)])
            for w in range(4):
                for rb in range(4):
                    row = 192 * w + 48 * rb
                    out_ref[w, 4 * rb + k] = total[row : row + 48].astype(bf16)
        col = pl.multiple_of(side * 384, LANES)
        total = dot(gated_t, low_ref[:, pl.ds(col, 384)])
        for k in range(2):
            for w in range(4):
                for rb in range(4):
                    row = 384 * w + 192 * k + 48 * rb
                    out_ref[w, 4 * rb + 2 + k] = total[row : row + 48].astype(bf16)


def early_grads(core, normed, dz, gated, low):
    shape = sds((4, 16, 48, 384), bf16)
    whole = pl.BlockSpec(memory_space=pltpu.VMEM)
    return call(
        early_grads_kernel,
        (shape, shape),
        in_specs=[pl.BlockSpec(memory_space=pltpu.SMEM)] + [whole] * 4,
        out_specs=[whole] * 2,
        flops=4 * ROWS * INNER * D,
        moved=7_000_000,
        name="early_grads",
    )(core, normed, dz, gated, low)


def within_back_kernel(vbc_ref, dy_ref, cum_ref, state_ref, dv_ref, dbc_ref, score, pile):
    b_part = vbc_ref[:, INNER : INNER + NSTATE]
    c_part = vbc_ref[:, INNER + NSTATE :]
    keep = iota((ROWS, ROWS), 0) <= iota((ROWS, ROWS), 1)
    score[...] = jnp.where(keep, dot_nt(b_part, c_part), 0.0)
    pile[...] = jnp.zeros_like(pile)
    cum = cum_ref[...]
    cum_t = jnp.transpose(cum)
    grown = jnp.exp(cum)
    left = iota((LANES, LANES), 1) < HDIM
    left_all = iota((ROWS, LANES), 1) < HDIM
    dc = jnp.zeros((ROWS, NSTATE), f32)
    for p in range(PAIRS):
        cols = slice(p * LANES, (p + 1) * LANES)
        values, dy = vbc_ref[:, cols], dy_ref[:, cols]
        tops, lows = [], []
        for side, h in enumerate((2 * p, 2 * p + 1)):
            col, row = cum[:, h : h + 1], cum_t[h : h + 1, :]
            mine = left_all if side == 0 else jnp.logical_not(left_all)
            own = jnp.where(mine, values.astype(f32), 0.0).astype(bf16)
            top = jnp.exp(jnp.minimum(row - col[0:LANES], 0.0))
            low = jnp.exp(jnp.minimum(row[:, LANES:] - col[LANES:], 0.0))
            tops.append(dot((top * score[0:LANES, :]).astype(bf16), dy))
            lows.append(dot((low * score[LANES:, LANES:]).astype(bf16), dy[LANES:]))
            pile[0:LANES, :] += top * dot_nt(own[0:LANES], dy)
            pile[LANES:, LANES:] += low * dot_nt(own[LANES:], dy[LANES:])
        dv_ref[0:LANES, cols] = jnp.where(left, tops[0], tops[1])
        dv_ref[LANES:, cols] = jnp.where(left, lows[0], lows[1])
        lifted = (dy.astype(f32) * pair_of(grown, p)).astype(bf16)
        dc = dc + dot(lifted, state_ref[cols, :])
    dscore = jnp.where(keep, pile[...], 0.0).astype(bf16)
    dbc_ref[:, 0:NSTATE] = dot(dscore, c_part)
    dbc_ref[:, NSTATE:] = dc + dot_tn(dscore, b_part)


def within_back(vbc, dy, cum, states):
    return call(
        within_back_kernel,
        (sds((ROWS, INNER), f32), sds((ROWS, 2 * NSTATE), f32)),
        scratch=[pltpu.VMEM((ROWS, ROWS), f32), pltpu.VMEM((ROWS, ROWS), f32)],
        flops=2 * HEADS * ROWS * ROWS * LANES * 6,
        moved=4_000_000,
        name="within_back",
    )(vbc, dy, cum, states)


def conv_back_kernel(
    later_ref, state_ref, dv_ref, dy_ref, vbc_ref, pre_ref, proj_ref, edge_ref, taps_ref, skip_ref,
    b_ref, cum_ref, step_ref, dt_ref, dbc_ref, row_ref, decay_ref, dtb_ref,
    pg_ref, edge_grad_ref, param_ref, ddt_ref, vec_ref,
    ext_in, ext_out, tail_keep, acc_b, acc_v, acc_x, acc_t, acc_s,
):
    k = pl.program_id(0)

    @pl.when(k == 0)
    def _():
        cum = cum_ref[...]
        tail_keep[...] = jnp.exp(cum[ROWS - 1 : ROWS] - cum)
        acc_b[...] = jnp.zeros_like(acc_b)
        acc_v[...] = jnp.zeros_like(acc_v)
        acc_x[...] = jnp.zeros_like(acc_x)
        acc_t[...] = jnp.zeros_like(acc_t)
        acc_s[...] = jnp.zeros_like(acc_s)
        ext_out[0:8] = jnp.zeros((8, 256), f32)
        ext_out[ROWS + 8 :] = jnp.zeros((8, 256), f32)

    pre = pre_ref[...]
    sig = sigmoid(pre)

    @pl.when(k < 6)
    def _():
        mask = head_mask(256, 4 * k)
        high, low = split2(step_ref[...])
        step = dot_nt(high, mask) + dot_nt(low, mask)
        high, low = split2(tail_keep[...])
        tail = dot_nt(high, mask) + dot_nt(low, mask)
        later = later_ref[...]
        value = vbc_ref[...].astype(f32)
        acc_b[...] += dot((value * tail).astype(bf16), later)
        from_state = tail * dot_nt(b_ref[...], later)
        dv = dv_ref[...] + from_state
        x = pre * sig
        high, low = split2(value * dv)
        acc_v[...] += dot(high, mask) + dot(low, mask)
        high, low = split2(x * dv)
        acc_x[...] += dot(high, mask) + dot(low, mask)
        sums = jnp.broadcast_to(jnp.sum(value * from_state, axis=0, keepdims=True), (16, 256))
        high, low = split2(sums)
        acc_t[...] += (dot(high, mask) + dot(low, mask))[0:8]
        high, low = split2(later.astype(f32) * state_ref[...].astype(f32))
        ones = jnp.ones((16, NSTATE), bf16)
        high, low = split2(dot_nt(ones, high) + dot_nt(ones, low))
        acc_s[...] += (dot(high, mask) + dot(low, mask))[0:8]
        ext_out[8 : 8 + ROWS] = step * dv + skip_ref[...] * dy_ref[...].astype(f32)

    @pl.when(k == 6)
    def _():
        ext_out[8 : 8 + ROWS, 0:NSTATE] = dbc_ref[:, 0:NSTATE] + acc_b[...]
        ext_out[8 : 8 + ROWS, NSTATE:] = dbc_ref[:, NSTATE:]
        inside = iota((ROWS, LANES), 1) < HEADS
        raw = jnp.where(inside, dt_ref[...], 0.0) + dtb_ref[...]
        rate = jnp.exp(decay_ref[...])
        log_decay = -step_ref[...] * rate
        whole = acc_t[0:1] + jnp.exp(cum_ref[ROWS - 1 : ROWS]) * acc_s[0:1]
        dlog = running_sum(row_ref[...] - acc_v[...], True) + whole
        dstep = acc_x[...] - dlog * rate
        ddt = jnp.where(inside, dstep * sigmoid(raw), 0.0)
        ddt_ref[...] = ddt.astype(bf16)
        vec_ref[0:1] = jnp.sum(jnp.where(inside, dlog * log_decay, 0.0), axis=0, keepdims=True)
        vec_ref[1:2] = jnp.sum(ddt, axis=0, keepdims=True)
        vec_ref[2:8] = jnp.zeros((6, LANES), f32)

    ds = ext_out[8 : 8 + ROWS] * (sig * (1.0 + pre * (1.0 - sig)))
    ext_out[8 : 8 + ROWS] = ds
    ext_in[0:8] = edge_ref[...]
    ext_in[8 : 8 + ROWS] = proj_ref[...]
    grad = taps_ref[3:4] * ds
    edge_grad = taps_ref[3:4] * ext_out[0:8]
    param_ref[3:4] = jnp.sum(ds * ext_in[8 : 8 + ROWS], axis=0, keepdims=True)
    for tap in range(WIDTH - 1):
        ahead = WIDTH - 1 - tap
        weight = taps_ref[tap : tap + 1]
        grad = grad + weight * ext_out[8 + ahead : 8 + ahead + ROWS]
        edge_grad = edge_grad + weight * ext_out[ahead : ahead + 8]
        param_ref[tap : tap + 1] = jnp.sum(ds * ext_in[5 + tap : 5 + tap + ROWS], axis=0, keepdims=True)
    param_ref[4:5] = jnp.sum(ds, axis=0, keepdims=True)
    param_ref[5:8] = jnp.zeros((3, 256), f32)
    pg_ref[...] = grad
    edge_grad_ref[...] = edge_grad


def conv_back(later, states, dv, dy, vbc, pre, proj, edge, taps, skip, cum, step, dbc, row, decay, dtb):
    block = 256
    upto = lambda k: jnp.minimum(k, 5)
    whole = lambda k: (0, 0)
    return call(
        conv_back_kernel,
        (
            sds((ROWS, CONV), f32),
            sds((8, CONV), f32),
            sds((8, CONV), f32),
            sds((ROWS, LANES), bf16),
            sds((8, LANES), f32),
        ),
        scratch=[
            pltpu.VMEM((ROWS + 8, block), f32),
            pltpu.VMEM((ROWS + 16, block), f32),
            pltpu.VMEM((ROWS, LANES), f32),
            pltpu.VMEM((ROWS, NSTATE), f32),
            pltpu.VMEM((ROWS, LANES), f32),
            pltpu.VMEM((ROWS, LANES), f32),
            pltpu.VMEM((8, LANES), f32),
            pltpu.VMEM((8, LANES), f32),
        ],
        grid=(7,),
        in_specs=[
            pl.BlockSpec((block, NSTATE), lambda k: (upto(k), 0)),
            pl.BlockSpec((block, NSTATE), lambda k: (upto(k), 0)),
            pl.BlockSpec((ROWS, block), lambda k: (0, upto(k))),
            pl.BlockSpec((ROWS, block), lambda k: (0, upto(k))),
            pl.BlockSpec((ROWS, block), lambda k: (0, k)),
            pl.BlockSpec((ROWS, block), lambda k: (0, k)),
            pl.BlockSpec((ROWS, block), lambda k: (0, 6 + k)),
            pl.BlockSpec((8, block), lambda k: (0, k)),
            pl.BlockSpec((WIDTH, block), lambda k: (0, k)),
            pl.BlockSpec((1, block), lambda k: (0, upto(k))),
            pl.BlockSpec((ROWS, NSTATE), lambda k: (0, 12)),
            pl.BlockSpec((ROWS, LANES), whole),
            pl.BlockSpec((ROWS, LANES), whole),
            pl.BlockSpec((ROWS, LANES), lambda k: (0, 26)),
            pl.BlockSpec((ROWS, 2 * NSTATE), whole),
            pl.BlockSpec((ROWS, LANES), whole),
            pl.BlockSpec((1, LANES), whole),
            pl.BlockSpec((1, LANES), whole),
        ],
        out_specs=[
            pl.BlockSpec((ROWS, block), lambda k: (0, k)),
            pl.BlockSpec((8, block), lambda k: (0, k)),
            pl.BlockSpec((8, block), lambda k: (0, k)),
            pl.BlockSpec((ROWS, LANES), whole),
            pl.BlockSpec((8, LANES), whole),
        ],
        flops=6 * ROWS * INNER * NSTATE,
        moved=12_000_000,
        name="conv_back",
    )(
        later, states, dv, dy, vbc, pre, proj, edge, taps, skip,
        vbc, cum, step, proj, dbc, row, decay, dtb,
    )


def norm_back_kernel(
    pg_ref, next_ref, dz_ref, ddt_ref, w_ref, x_ref, gain_ref, grad_ref,
    low_ref, out_ref, dgain_ref,
):
    low_ref[0 : ROWS - 16] = pg_ref[0 : ROWS - 16].astype(bf16)
    last = pg_ref[ROWS - 16 :]
    low_ref[ROWS - 16 :] = jnp.concatenate([last[0:8], last[8:16] + next_ref[...]]).astype(bf16)
    back = dot_nt(dz_ref[...], w_ref[:, 0:INNER])
    back = back + dot_nt(low_ref[...], w_ref[:, INNER : INNER + CONV])
    back = back + dot_nt(ddt_ref[:, 0:HEADS], w_ref[:, INNER + CONV : PROJ])
    x = x_ref[...].astype(f32)
    scale = lax.rsqrt(jnp.mean(x * x, axis=-1, keepdims=True) + EPS)
    dgain_ref[...] = jnp.sum(back * x * scale, axis=0, keepdims=True)
    scaled = back * gain_ref[...]
    pull = scale * scale * scale * jnp.mean(scaled * x, axis=-1, keepdims=True)
    out_ref[...] = grad_ref[...].astype(f32) + scaled * scale - x * pull


def norm_back(pg, following, dz, ddt, weight, x, gain, grad):
    return call(
        norm_back_kernel,
        (sds((ROWS, CONV), bf16), sds((ROWS, D), f32), sds((1, D), f32)),
        flops=2 * ROWS * D * PROJ,
        moved=11_000_000,
        name="norm_back",
    )(pg, following, dz, ddt, weight, x, gain, grad)


def late_grads_kernel(
    core_ref, normed_ref, low_ref, ddt_ref, dgain_in_ref, dgain_out_ref, param_ref, vec_ref, dskip_ref,
    keep_ref, send_ref, small,
):
    core = core_ref[0]
    small[...] = jnp.zeros_like(small)
    line = 0
    for ref, first, count in ((dgain_in_ref, 0, 6), (dgain_out_ref, 0, 12)):
        for i in range(count):
            small[line : line + 1, :] = ref[first : first + 1, LANES * i : LANES * i + LANES]
            line += 1
    for tap in range(WIDTH + 1):
        for i in range(CONV // LANES):
            small[line : line + 1, :] = param_ref[tap : tap + 1, LANES * i : LANES * i + LANES]
            line += 1
    vec = vec_ref[...]
    lane = iota((8, LANES), 1)
    decay = jnp.where(lane < HEADS, jnp.broadcast_to(vec[0:1], (8, LANES)), 0.0)
    dtb = jnp.where(lane < HEADS, jnp.broadcast_to(vec[1:2], (8, LANES)), 0.0)
    skip = jnp.where(lane < HEADS, dskip_ref[...], 0.0)
    joined = decay + pltpu.roll(dtb, HEADS, 1) + pltpu.roll(skip, 2 * HEADS, 1)
    small[line : line + 1, :] = joined[0:1]

    normed_t = jnp.transpose(normed_ref[...])

    def place(out_ref, k, lanes, total):
        for w in range(4):
            for rb in range(4):
                row = 192 * w + 48 * rb
                out_ref[w, 4 * rb + k, :, lanes] = total[row : row + 48].astype(bf16)

    for out_ref, side in ((keep_ref, core), (send_ref, 1 - core)):
        for k in range(3):
            col = pl.multiple_of((2 * k + side) * 256, LANES)
            place(out_ref, k, slice(0, 256), dot(normed_t, low_ref[:, pl.ds(col, 256)]))

        @pl.when(side == 0)
        def _(out_ref=out_ref):
            place(out_ref, 3, slice(0, 256), dot(normed_t, low_ref[:, 1536:1792]))

        @pl.when(side == 1)
        def _(out_ref=out_ref):
            place(out_ref, 3, slice(0, 128), dot(normed_t, ddt_ref[...]))
            for w in range(4):
                for rb in range(4):
                    if rb < 2:
                        block = small[48 * rb : 48 * rb + 48, :]
                    else:
                        block = jnp.zeros((48, LANES), f32)
                    out_ref[w, 4 * rb + 3, :, 128:256] = block.astype(bf16)


def late_grads(core, normed, low, ddt, dgain_in, dgain_out, param, vec, dskip):
    shape = sds((4, 16, 48, 256), bf16)
    whole = pl.BlockSpec(memory_space=pltpu.VMEM)
    return call(
        late_grads_kernel,
        (shape, shape),
        scratch=[pltpu.VMEM((96, LANES), f32)],
        in_specs=[pl.BlockSpec(memory_space=pltpu.SMEM)] + [whole] * 8,
        out_specs=[whole] * 2,
        flops=2 * ROWS * D * CONV,
        moved=5_000_000,
        name="late_grads",
    )(core, normed, low, ddt, dgain_in, dgain_out, param, vec, dskip)


def adam_step(weight, moment, second, gradient, learn_rate, weight_decay):
    new_moment = 0.9 * moment + 0.1 * gradient
    new_second = 0.95 * second + 0.05 * gradient * gradient
    corrected = new_moment / (1.0 - 0.9**STEP) / (jnp.sqrt(new_second / (1.0 - 0.95**STEP)) + 1e-08)
    return (new_moment, new_second, weight - learn_rate * (corrected + weight_decay * weight))


def adam_kernel(
    core_ref, early_own, early_other, late_own, late_other, in_w, in_m, in_v, out_w, out_m, out_v, *refs
):
    in_outs, out_outs, token = refs[-7:-4], refs[-4:-1], refs[-1]
    token[...] = jnp.zeros_like(token)
    first = core_ref[0] == 0

    def sides(own, other, k):
        a, b = own[0, k].astype(f32), other[0, k].astype(f32)
        return jnp.where(first, a, b), jnp.where(first, b, a)

    def update(ins, outs, spot, grad, rate):
        new_m, new_v, new_w = adam_step(*(ref[spot] for ref in ins), grad, rate, 0.1)
        for out, new in zip(outs, (new_w, new_m, new_v), strict=True):
            out[spot] = new

    def update_in(col, width, grad):
        update((in_w, in_m, in_v), in_outs, (0, slice(None), slice(col, col + width)), grad, 0.03)

    for k in range(4):
        for side, grad in enumerate(sides(early_own, early_other, k)):
            if k < 2:
                update_in(384 * (2 * k + side), 384, grad)
            else:
                spot = (0, k - 2, slice(None), slice(384 * side, 384 * side + 384))
                update((out_w, out_m, out_v), out_outs, spot, grad, 0.02)
        for side, grad in enumerate(sides(late_own, late_other, k)):
            if 2 * k + side < 7:
                update_in(INNER + 256 * (2 * k + side), 256, grad)
            else:
                update_in(INNER + CONV, HEADS, grad[:, 0:HEADS])


def adam(core, early, early_at, late, late_at, in_state, out_state, layer, before):
    rows = 16
    in_block = pl.BlockSpec((1, rows, PROJ), lambda r: (layer, r, 0))
    out_block = pl.BlockSpec((1, 2, rows, D), lambda r: (layer, 0, r, 0))
    early_block = pl.BlockSpec((1, 4, rows, 384), lambda r: (r // 3, 0, r % 3, early_at))
    late_block = pl.BlockSpec((1, 4, rows, 256), lambda r: (r // 3, 0, r % 3, late_at))
    in_shape = sds((2, 192, PROJ), f32)
    out_shape = sds((2, 2, 192, D), f32)
    held = () if before is None else tuple(before[:6])
    return call(
        adam_kernel,
        (in_shape,) * 3 + (out_shape,) * 3 + (sds((8, LANES), bf16),),
        grid=(192 // rows,),
        in_specs=[pl.BlockSpec(memory_space=pltpu.SMEM)]
        + [early_block] * 2
        + [late_block] * 2
        + [in_block] * 3
        + [out_block] * 3
        + [pl.BlockSpec(memory_space=pl.ANY)] * len(held),
        out_specs=[in_block] * 3 + [out_block] * 3 + [pl.BlockSpec((8, LANES), lambda r: (0, 0))],
        input_output_aliases={11 + n: n for n in range(len(held))},
        moved=24_000_000,
        name="adam",
    )(core, *early, *late, *in_state, *out_state, *held)


def next_in_sequence(rows, step):
    route = [(i, i + step) for i in range(32) if 0 <= i + step < 32]
    return lax.ppermute(rows, PLANE, route)


def exchange(blocks):
    return lax.all_to_all(blocks, PLANE, 0, 0, tiled=True)


def turned(block, axis, step):
    return lax.ppermute(block, axis, [(i, (i + step) % 4) for i in range(4)])


def swapped(block):
    return lax.ppermute(block, "core", [(0, 1), (1, 0)])


def assemble_kernel(place_ref, *refs):
    pieces, full_ref = refs[:-1], refs[-1]
    me, core = place_ref[0], place_ref[1]
    full_ref[pl.ds(pl.multiple_of(me * 192, 48), 192), :] = pieces[0][...]
    for side in range(2):
        half = core if side == 0 else 1 - core
        for n, (turn, first, count) in enumerate(((3, 0, 96), (1, 0, 96), (2, 0, 48), (2, 48, 48))):
            row = lax.rem(me + turn, 4) * 192 + half * 96 + first
            spot = pl.ds(pl.multiple_of(row, 48), count)
            full_ref[spot, :] = pieces[1 + 4 * side + n][0:count, :]


def gather_start(shard, rider=None):
    half = lax.dynamic_slice_in_dim(shard, 96 * lax.axis_index("core"), 96, 0).astype(bf16)
    if rider is not None:
        half = jnp.concatenate([half, rider])
    return turned(half, "wt", 1), turned(half, "wt", -1)


def gather_far(before, after):
    return turned(before[:48], "wt", 1), turned(after[48:], "wt", -1)


def gather_end(shard, mine):
    place = jnp.stack([lax.axis_index("wt"), lax.axis_index("core")]).astype(jnp.int32)
    rows = [192] + [piece.shape[0] for piece in mine] * 2
    return call(
        assemble_kernel,
        sds((D, PROJ), bf16),
        in_specs=[pl.BlockSpec(memory_space=pltpu.SMEM)] + [pl.BlockSpec((count, PROJ)) for count in rows],
        out_specs=pl.BlockSpec((D, PROJ)),
        moved=10_000_000,
        name="assemble",
    )(place, shard, *mine, *[swapped(piece) for piece in mine])


def tie(*values):
    return lax.optimization_barrier(values)


def paired(keep, send):
    return (keep.astype(f32) + swapped(send).astype(f32)).astype(bf16)


def summed(parts):
    return jnp.sum(parts.astype(f32), axis=0).astype(bf16)


def over_wt(pieces):
    return lax.psum_scatter(pieces, "wt", scatter_dimension=0, tiled=True)[0]


def over_plane(part):
    return summed(lax.all_to_all(part, ("x", "z"), 0, 0, tiled=True))


def spread(piece):
    pieces = jnp.broadcast_to(piece[None], (16, *piece.shape))
    own = lax.all_to_all(pieces, ("x", "z"), 0, 0, tiled=True).reshape(4, 4, *piece.shape)
    return own, swapped(own)


def shards(
    tokens, in_w, in_m, in_v, out_w, out_m, out_v, small_params, small_m, small_v, cotangent
):
    core = lax.axis_index("core").astype(jnp.int32).reshape(1)
    tokens = tokens[0]
    cotangent = cotangent[0]
    in_low, out_low = in_w.astype(bf16), out_w.astype(bf16)
    rider = jnp.pad(small_params.astype(bf16), ((0, 6), (0, PROJ - VEC // 4)))
    near = gather_start(in_w[0], rider)
    far = gather_far(*near)
    *far, out_now = tie(*far, out_low[0])
    in_full = [gather_end(in_low[0], (*near, *far)), None]
    out_full = [lax.all_gather(out_now, "wt", axis=0, tiled=True), None]
    riders = jnp.stack([rider, near[1][96:], far[1][48:], near[0][96:]])
    riders = riders[lax.rem(jnp.arange(4) + 4 - lax.axis_index("wt"), 4)]
    small_full = jnp.swapaxes(riders[:, :2, : VEC // 4], 0, 1).reshape(2, VEC).astype(f32)

    def heads_row(first):
        return jnp.pad(small_full[:, first : first + HEADS], ((0, 0), (0, LANES - HEADS)))

    gain_in = small_full[:, :D]
    gain_out = small_full[:, D : D + INNER]
    taps = small_full[:, 2304:9472].reshape(2, WIDTH, CONV)
    bias = small_full[:, 9472:11264]
    decay = heads_row(11264)
    dtb = heads_row(11264 + HEADS)
    skip = jnp.repeat(small_full[:, 11264 + 2 * HEADS : VEC], HDIM, axis=1)

    hidden = tokens
    saved = []
    for layer in range(2):
        row = slice(layer, layer + 1)
        edge = next_in_sequence(hidden[ROWS - 8 :], 1)
        normed, proj = project(hidden, gain_in[row], in_full[layer])
        if layer == 0:
            normed, shard = tie(normed, in_w[1])
            near = gather_start(shard)
        pre, edge_in, vbc, cum, step, pay = conv_states(
            edge, gain_in[row], in_full[layer], proj, taps[layer], bias[row], decay[row], dtb[row]
        )
        slices = exchange(pay)
        yw = within(vbc, cum)
        if layer == 0:
            slices, *near = tie(slices, *near)
            far = gather_far(*near)
        scanned, chain = scan_states(slices)
        states = exchange(scanned)
        if layer == 0:
            states, yw, *far = tie(states, yw, *far)
        states = states.reshape(INNER, NSTATE)
        after, y, gated = output_part(
            yw, vbc, cum, pre, proj, states, hidden, out_full[layer], gain_out[row], skip[row]
        )
        saved.append((hidden, normed, proj, pre, edge_in, vbc, cum, step, chain, states, y, gated))
        hidden = after
        if layer == 0:
            after, out_now = tie(after, out_low[1])
            hidden = after
            in_full[1] = gather_end(in_low[1], (*near, *far))
            out_full[1] = lax.all_gather(out_now, "wt", axis=0, tiled=True)

    grad = cotangent
    early_part, late_part = [None, None], [None, None]
    for layer in (1, 0):
        row = slice(layer, layer + 1)
        start, normed, proj, pre, edge_in, vbc, cum, step, chain, states, y, gated = saved[layer]
        low, dz, dy, local, rows_sum, dgain_out, dskip = gate_back(
            grad, out_full[layer], y, proj, pre, vbc, cum, gain_out[row], skip[row]
        )
        slices = exchange(local)
        keep, send = early_grads(core, normed, dz, gated, low)
        dv, dbc = within_back(vbc, dy, cum, states)
        slices, keep, send, dv, dbc = tie(slices, keep, send, dv, dbc)
        scanned = scan_back(slices, chain)
        later = exchange(scanned)
        early = paired(keep, send)
        later, early = tie(later, early)
        later = later.reshape(INNER, NSTATE)
        early_part[layer] = over_wt(early)
        if layer == 0:
            upper = jnp.concatenate([early_part[1], late_part[1]], axis=2)
            later, upper = tie(later, upper)
            upper_sum = over_plane(upper)
        pg, edge_grad, param, ddt, vec = conv_back(
            later, states, dv, dy, vbc, pre, proj, edge_in, taps[layer], skip[row],
            cum, step, dbc, rows_sum, decay[row], dtb[row],
        )
        following = next_in_sequence(edge_grad, -1)
        pg_low, grad, dgain_in = norm_back(
            pg, following, dz, ddt, in_full[layer], start, gain_in[row], grad
        )
        if layer == 0:
            pg_low, upper_sum = tie(pg_low, upper_sum)
        late = paired(*late_grads(core, normed, pg_low, ddt, dgain_in, dgain_out, param, vec, dskip))
        late_part[layer] = over_wt(late)

    early_sum = over_plane(early_part[0])
    first_all = spread(jnp.concatenate([upper_sum[:, :384], early_sum, upper_sum[:, 384:]], axis=1))
    split = lambda a: a.reshape(2, 2, 192, D)
    in_state, out_state = (in_w, in_m, in_v), (split(out_w), split(out_m), split(out_v))
    news = adam(core, first_all, 0, first_all, 3, in_state, out_state, 1, None)
    last_part, first_all = tie(late_part[0], first_all)
    last_all = spread(over_plane(last_part) + news[6][0, 0])
    news = adam(core, first_all, 1, last_all, 0, in_state, out_state, 0, news)
    small_total = jnp.stack(
        [
            jnp.where(core[0] == 0, other, own)[0:2, 3, :, at + LANES : at + 2 * LANES].reshape(96 * LANES)[:VEC]
            for (own, other), at in ((last_all, 0), (first_all, 768))
        ]
    )
    width = VEC // 4
    small_total = lax.dynamic_slice_in_dim(
        small_total.astype(f32), lax.axis_index("wt") * width, width, 1
    )
    new_small = adam_step(small_params, small_m, small_v, small_total, 0.2, 0.0)
    return (
        hidden[None],
        grad[None],
        news[1],
        news[2],
        news[0],
        news[4].reshape(2, 384, D),
        news[5].reshape(2, 384, D),
        news[3].reshape(2, 384, D),
        *new_small,
    )


def solution(mesh):
    fine = Mesh(mesh.devices.reshape(4, 4, 2, 4), ("x", "z", "core", "wt"))
    rows = P("wt", PLANE, None)
    held = P(None, "wt", None)
    flat = P(None, "wt")
    return jax.shard_map(
        shards,
        mesh=fine,
        in_specs=(rows, held, held, held, held, held, held, flat, flat, flat, rows),
        out_specs=(rows, rows, held, held, held, held, held, held, flat, flat, flat),
        check_vma=False,
    )
```

```python
import functools

import jax
import jax.numpy as jnp
from jax import lax
from jax.experimental import pallas as pl
from jax.experimental.pallas import tpu as pltpu
from jax.sharding import Mesh
from jax.sharding import PartitionSpec as P

D = 768
HEADS = 24
HDIM = 64
NSTATE = 128
WIDTH = 4
STEP = 10
INNER = 1536
CONV = 1792
PROJ = 3352
VEC = 11336
ROWS = 256
EPS = 1e-05
PAIRS = HEADS // 2
LANES = 128
PLANE = ("x", "z", "core")

bf16 = jnp.bfloat16
f32 = jnp.float32
MIB = 1024 * 1024


def call(kernel, outs, scratch=(), grid=(), in_specs=None, out_specs=None, flops=0, moved=0, vmem=60, **kw):
    params = pltpu.CompilerParams(vmem_limit_bytes=vmem * MIB)
    extra = {}
    if in_specs is not None:
        extra["in_specs"] = in_specs
        extra["out_specs"] = out_specs
    return pl.pallas_call(
        kernel,
        out_shape=outs,
        grid=grid,
        scratch_shapes=list(scratch),
        compiler_params=params,
        cost_estimate=pl.CostEstimate(flops=flops, bytes_accessed=moved, transcendentals=0),
        **extra,
        **kw,
    )


def sds(shape, dtype):
    return jax.ShapeDtypeStruct(shape, dtype)


def dot(a, b):
    return lax.dot_general(a, b, (((1,), (0,)), ((), ())), preferred_element_type=f32)


def dot_nt(a, b):
    return lax.dot_general(a, b, (((1,), (1,)), ((), ())), preferred_element_type=f32)


def dot_tn(a, b):
    return lax.dot_general(a, b, (((0,), (0,)), ((), ())), preferred_element_type=f32)


def split2(v):
    high = v.astype(bf16)
    return high, (v - high.astype(f32)).astype(bf16)


def split3(v):
    high = v.astype(bf16)
    rest = v - high.astype(f32)
    mid = rest.astype(bf16)
    return high, mid, (rest - mid.astype(f32)).astype(bf16)


def iota(shape, dim):
    return lax.broadcasted_iota(jnp.int32, shape, dim)


def sigmoid(v):
    return 0.5 * jnp.tanh(0.5 * v) + 0.5


def silu(v):
    return v * sigmoid(v)


def softplus(v):
    return jnp.maximum(v, 0.0) + jnp.log1p(jnp.exp(-jnp.abs(v)))


def pair_of(v, p):
    rows = v.shape[0]
    left = jnp.broadcast_to(v[:, 2 * p : 2 * p + 1], (rows, LANES))
    right = jnp.broadcast_to(v[:, 2 * p + 1 : 2 * p + 2], (rows, LANES))
    return jnp.where(iota((rows, LANES), 1) < HDIM, left, right)


def head_mask(columns, first_head):
    return ((iota((columns, LANES), 0) >> 6) + first_head == iota((columns, LANES), 1)).astype(bf16)


def running_sum(v, reverse):
    rows, cols = iota((ROWS, ROWS), 0), iota((ROWS, ROWS), 1)
    tri = ((cols >= rows) if reverse else (cols <= rows)).astype(bf16)
    high, mid, low = split3(v)
    return dot(tri, high) + dot(tri, mid) + dot(tri, low)


class Mover:
    def __init__(self, sems):
        self.sems = sems
        self.count = 0
        self.out = []

    def take(self, src, dst):
        copy = pltpu.make_async_copy(src, dst, self.sems.at[self.count])
        self.count += 1
        copy.start()
        return copy

    def give(self, src, dst):
        self.out.append(self.take(src, dst))

    def finish(self):
        for copy in self.out:
            copy.wait()


def wait_all(copies):
    for copy in copies:
        copy.wait()


def moved_call(kernel, ins, outs, scratch, copies, smem=0, **kw):
    anywhere = pl.BlockSpec(memory_space=pl.ANY)
    return call(
        kernel,
        outs,
        scratch=[pltpu.VMEM(s.shape, s.dtype) for s in scratch] + [pltpu.SemaphoreType.DMA((copies,))],
        in_specs=[pl.BlockSpec(memory_space=pltpu.SMEM)] * smem + [anywhere] * (len(ins) - smem),
        out_specs=[anywhere] * len(outs),
        **kw,
    )(*ins)


def project_kernel(
    place_ref, x_hbm, gain_hbm, *refs
):
    pieces = refs[:9]
    w_hbm, wd_hbm, normed_hbm, z_hbm, cin_hbm, dt_hbm = refs[9:15]
    x, gain, w, wd, normed, z, cin, dt, sems = refs[15:]
    move = Mover(sems)
    first = [move.take(x_hbm, x), move.take(gain_hbm, gain)]
    me, core = place_ref[0], place_ref[1]
    spot = pl.ds(pl.multiple_of(me * 192, 48), 192)
    parts = [move.take(pieces[0], w.at[spot])]
    for side in range(2):
        half = core if side == 0 else 1 - core
        for n, (turn, start, count) in enumerate(((3, 0, 96), (1, 0, 96), (2, 0, 48), (2, 48, 48))):
            row = lax.rem(me + turn, 4) * 192 + half * 96 + start
            spot = pl.ds(pl.multiple_of(row, 48), count)
            parts.append(move.take(pieces[1 + 4 * side + n].at[pl.ds(0, count)], w.at[spot]))
    wait_all(first)
    rows = x[...].astype(f32)
    scale = lax.rsqrt(jnp.mean(rows * rows, axis=-1, keepdims=True) + EPS)
    normed[...] = (rows * scale * gain[...]).astype(bf16)
    move.give(normed, normed_hbm)
    wait_all(parts)
    move.give(w, w_hbm)
    wd[...] = jnp.zeros_like(wd)
    wd[:, 0:HEADS] = w[:, INNER + CONV : PROJ]
    move.give(wd, wd_hbm)
    dt[...] = dot(normed[...], wd[...])
    move.give(dt, dt_hbm)
    for k in (6, 0, 1, 2, 3, 4, 5):
        cols = slice(256 * k, 256 * k + 256)
        cin[:, cols] = dot(normed[...], w[:, INNER + 256 * k : INNER + 256 * k + 256])
        if k % 2 == 0 and k < 6:
            continue
        span = pl.ds(1536, 256) if k == 6 else pl.ds(256 * k - 256, 512)
        move.give(cin.at[:, span], cin_hbm.at[:, span])
    for k in range(3):
        cols = slice(512 * k, 512 * k + 512)
        z[:, cols] = dot(normed[...], w[:, cols])
        move.give(z.at[:, pl.ds(512 * k, 512)], z_hbm.at[:, pl.ds(512 * k, 512)])
    move.finish()


def project(place, x, gain, pieces):
    return moved_call(
        project_kernel,
        (place, x, gain, *pieces),
        (
            sds((D, PROJ), bf16),
            sds((D, LANES), bf16),
            sds((ROWS, D), bf16),
            sds((ROWS, INNER), f32),
            sds((ROWS, CONV), f32),
            sds((ROWS, LANES), f32),
        ),
        (
            sds((ROWS, D), x.dtype),
            sds((1, D), f32),
            sds((D, PROJ), bf16),
            sds((D, LANES), bf16),
            sds((ROWS, D), bf16),
            sds((ROWS, INNER), f32),
            sds((ROWS, CONV), f32),
            sds((ROWS, LANES), f32),
        ),
        24,
        smem=1,
        flops=2 * ROWS * D * PROJ,
        moved=14_000_000,
        name="project",
    )


def conv_kernel(
    edge_hbm, gain_hbm, w_hbm, cin_hbm, dt_hbm, taps_hbm, bias_hbm, decay_hbm, dtb_hbm,
    pre_hbm, edge_out_hbm, vbc_hbm, cum_hbm, step_hbm, pay_hbm,
    edge, gain, w, cin, dt, taps, bias, decay, dtb,
    pre, edge_in, vbc, cum_ref, step_ref, pay, ext, states, sems,
):
    move = Mover(sems)
    small = [
        move.take(src, dst)
        for src, dst in (
            (dt_hbm, dt), (dtb_hbm, dtb), (decay_hbm, decay), (edge_hbm, edge), (gain_hbm, gain),
            (taps_hbm, taps), (bias_hbm, bias),
        )
    ]
    chunks = [(1536, 256), (0, 512), (512, 512), (1024, 512)]
    copies = []
    for start, count in chunks:
        copies.append(
            (
                move.take(w_hbm.at[:, pl.ds(INNER + start, count)], w.at[:, pl.ds(start, count)]),
                move.take(cin_hbm.at[:, pl.ds(start, count)], cin.at[:, pl.ds(start, count)]),
            )
        )
    wait_all(small)
    inside = iota((ROWS, LANES), 1) < HEADS
    step = jnp.where(inside, softplus(dt[...] + dtb[...]), 0.0)
    cum = running_sum(-step * jnp.exp(decay[...]), False)
    step_ref[...] = step
    cum_ref[...] = cum
    move.give(step_ref, step_hbm)
    move.give(cum_ref, cum_hbm)
    tail = jnp.exp(cum[ROWS - 1 : ROWS] - cum)
    rows = edge[...].astype(f32)
    scale = lax.rsqrt(jnp.mean(rows * rows, axis=-1, keepdims=True) + EPS)
    before = rows * scale * gain[...]
    before = jnp.concatenate([before, jnp.zeros_like(before)]).astype(bf16)
    b_part = None
    for (start, count), arrived in zip(chunks, copies, strict=True):
        wait_all(arrived)
        edge_in[:, start : start + count] = dot(before, w[:, start : start + count])[0:8]
        for block in range(start // LANES, (start + count) // LANES):
            cols = slice(block * LANES, (block + 1) * LANES)
            ext[block, 0:8] = edge_in[:, cols]
            ext[block, 8 : 8 + ROWS] = cin[:, cols]
            total = bias[:, cols] + taps[3:4, cols] * cin[:, cols]
            for tap in range(WIDTH - 1):
                total = total + taps[tap : tap + 1, cols] * ext[block, 5 + tap : 5 + tap + ROWS]
            pre[:, cols] = total
            out = total * sigmoid(total)
            if block >= PAIRS:
                vbc[:, cols] = out.astype(bf16)
                if block == PAIRS:
                    b_part = out.astype(bf16)
                continue
            value = out * pair_of(step, block)
            vbc[:, cols] = value.astype(bf16)
            tailed = (value * pair_of(tail, block)).astype(bf16)
            states[cols, :] = dot_tn(tailed, b_part)
        span = pl.ds(start, count)
        move.give(pre.at[:, span], pre_hbm.at[:, span])
        move.give(vbc.at[:, span], vbc_hbm.at[:, span])
    move.give(edge_in, edge_out_hbm)
    total_log = cum[ROWS - 1 : ROWS, :]
    head = (iota((32, LANES), 0) * 48 + iota((32, LANES), 1)) >> 6
    logs = jnp.zeros((32, LANES), f32)
    for h in range(HEADS):
        logs = jnp.where(head == h, total_log[:, h : h + 1], logs)
    row16 = iota((16, LANES), 0)
    for piece in range(32):
        pay[piece, 0:48, :] = states[48 * piece : 48 * piece + 48, :].astype(bf16)
        line = logs[piece : piece + 1, :]
        high = line.astype(bf16).astype(f32)
        extra = jnp.where(row16 == 0, high, jnp.where(row16 == 1, line - high, 0.0))
        pay[piece, 48:64, :] = extra.astype(bf16)
    move.give(pay, pay_hbm)
    move.finish()


def conv_states(edge, gain, weight, cin, dt, taps, bias, decay, dtb):
    outs = (
        sds((ROWS, CONV), f32),
        sds((8, CONV), f32),
        sds((ROWS, CONV), bf16),
        sds((ROWS, LANES), f32),
        sds((ROWS, LANES), f32),
        sds((32, 64, LANES), bf16),
    )
    return moved_call(
        conv_kernel,
        (edge, gain, weight, cin, dt, taps, bias, decay, dtb),
        outs,
        (
            sds((8, D), edge.dtype),
            sds((1, D), f32),
            sds((D, CONV), bf16),
            sds((ROWS, CONV), f32),
            sds((ROWS, LANES), f32),
            sds((WIDTH, CONV), f32),
            sds((1, CONV), f32),
            sds((1, LANES), f32),
            sds((1, LANES), f32),
            *outs,
            sds((CONV // LANES, ROWS + 8, LANES), f32),
            sds((INNER, NSTATE), f32),
        ),
        28,
        flops=2 * ROWS * INNER * NSTATE + 2 * 16 * D * CONV,
        moved=9_000_000,
        name="conv_states",
    )


def within_kernel(vbc_ref, cum_ref, y_ref, score):
    b_part = vbc_ref[:, INNER : INNER + NSTATE]
    c_part = vbc_ref[:, INNER + NSTATE :]
    keep = iota((ROWS, ROWS), 0) >= iota((ROWS, ROWS), 1)
    score[...] = jnp.where(keep, dot_nt(c_part, b_part), 0.0)
    cum = cum_ref[...]
    cum_t = jnp.transpose(cum)
    left = iota((LANES, LANES), 1) < HDIM
    for p in range(PAIRS):
        values = vbc_ref[:, p * LANES : (p + 1) * LANES]
        tops, lows = [], []
        for h in (2 * p, 2 * p + 1):
            col, row = cum[:, h : h + 1], cum_t[h : h + 1, :]
            top = jnp.exp(jnp.minimum(col[0:LANES] - row[:, 0:LANES], 0.0)) * score[0:LANES, 0:LANES]
            tops.append(dot(top.astype(bf16), values[0:LANES]))
            low = jnp.exp(jnp.minimum(col[LANES:] - row, 0.0)) * score[LANES:, :]
            lows.append(dot(low.astype(bf16), values))
        y_ref[0:LANES, p * LANES : (p + 1) * LANES] = jnp.where(left, tops[0], tops[1])
        y_ref[LANES:, p * LANES : (p + 1) * LANES] = jnp.where(left, lows[0], lows[1])


def within(vbc, cum):
    return call(
        within_kernel,
        sds((ROWS, INNER), f32),
        scratch=[pltpu.VMEM((ROWS, ROWS), f32)],
        flops=2 * HEADS * ROWS * ROWS * LANES * 4,
        moved=3_000_000,
        name="within",
    )(vbc, cum)


def scan_kernel(pay_ref, out_ref, decay_ref, logs):
    logs[...] = jnp.zeros_like(logs)
    for s in range(32):
        extra = pay_ref[s, 48:64, :].astype(f32)
        logs[s : s + 1, :] = extra[0:1] + extra[1:2]
    decay = jnp.exp(jnp.transpose(logs[...]))
    decay_ref[...] = decay
    carry = jnp.zeros((48, LANES), f32)
    for s in range(32):
        out_ref[s] = carry.astype(bf16)
        carry = decay[0:48, s : s + 1] * carry + pay_ref[s, 0:48, :].astype(f32)


def scan_states(pay):
    return call(
        scan_kernel,
        (sds((32, 48, LANES), bf16), sds((LANES, LANES), f32)),
        scratch=[pltpu.VMEM((LANES, LANES), f32)],
        moved=1_000_000,
        name="scan_states",
    )(pay)


def scan_back_kernel(grad_ref, decay_ref, out_ref):
    decay = decay_ref[...]
    carry = jnp.zeros((48, LANES), f32)
    for s in reversed(range(32)):
        out_ref[s] = carry.astype(bf16)
        carry = decay[0:48, s : s + 1] * carry + grad_ref[s].astype(f32)


def scan_back(grad, decay):
    return call(
        scan_back_kernel, sds((32, 48, LANES), bf16), moved=800_000, name="scan_back"
    )(grad, decay)


def output_kernel(
    yw_hbm, vbc_hbm, cum_hbm, pre_hbm, z_hbm, state_hbm, hid_hbm, w_hbm, gain_hbm, skip_hbm,
    hid_out_hbm, y_hbm, gated_hbm,
    yw, c_part, cum, pre, z, state, hid, w, gain, skip, hid_out, y_ref, gated, gate, sems,
):
    move = Mover(sems)
    small = [
        move.take(src, dst)
        for src, dst in ((cum_hbm, cum), (skip_hbm, skip), (gain_hbm, gain), (state_hbm, state))
    ]
    small.append(move.take(vbc_hbm.at[:, pl.ds(INNER + NSTATE, NSTATE)], c_part))
    copies = []
    for k in range(3):
        span = pl.ds(512 * k, 512)
        copies.append(
            [move.take(src.at[:, span], dst.at[:, span]) for src, dst in ((yw_hbm, yw), (pre_hbm, pre), (z_hbm, z))]
        )
    last = [move.take(w_hbm, w), move.take(hid_hbm, hid)]
    wait_all(small)
    grown = jnp.exp(cum[...])
    square = jnp.zeros((ROWS, 1), f32)
    for p in range(PAIRS):
        if p % 4 == 0:
            wait_all(copies[p // 4])
        cols = slice(p * LANES, (p + 1) * LANES)
        y = yw[:, cols] + dot_nt(c_part[...], state[cols, :]) * pair_of(grown, p)
        y_ref[:, cols] = y
        u = (y + skip[:, cols] * silu(pre[:, cols])) * silu(z[:, cols])
        gate[:, cols] = u
        square = square + jnp.sum(u * u, axis=-1, keepdims=True)
        if p % 4 == 3:
            span = pl.ds(512 * (p // 4), 512)
            move.give(y_ref.at[:, span], y_hbm.at[:, span])
    scale = lax.rsqrt(square * (1.0 / INNER) + EPS)
    gated[...] = (gate[...] * scale * gain[...]).astype(bf16)
    move.give(gated, gated_hbm)
    wait_all(last)
    for k in range(3):
        cols = slice(256 * k, 256 * k + 256)
        hid_out[:, cols] = hid[:, cols].astype(f32) + dot(gated[...], w[:, cols])
        move.give(hid_out.at[:, pl.ds(256 * k, 256)], hid_out_hbm.at[:, pl.ds(256 * k, 256)])
    move.finish()


def output_part(yw, vbc, cum, pre, z, states, hidden, weight, gain, skip):
    outs = (sds((ROWS, D), f32), sds((ROWS, INNER), f32), sds((ROWS, INNER), bf16))
    return moved_call(
        output_kernel,
        (yw, vbc, cum, pre, z, states, hidden, weight, gain, skip),
        outs,
        (
            sds((ROWS, INNER), f32),
            sds((ROWS, NSTATE), bf16),
            sds((ROWS, LANES), f32),
            sds((ROWS, INNER), f32),
            sds((ROWS, INNER), f32),
            sds((INNER, NSTATE), bf16),
            sds((ROWS, D), hidden.dtype),
            sds((INNER, D), bf16),
            sds((1, INNER), f32),
            sds((1, INNER), f32),
            *outs,
            sds((ROWS, INNER), f32),
        ),
        24,
        flops=2 * ROWS * INNER * (D + LANES),
        moved=10_000_000,
        name="output_part",
    )


def gate_back_kernel(
    grad_hbm, w_hbm, y_hbm, z_hbm, pre_hbm, vbc_hbm, cum_hbm, gain_hbm, skip_hbm,
    low_hbm, dz_hbm, dy_hbm, local_hbm, row_hbm, dgain_hbm, dskip_hbm,
    grad, w, y_ref, z_ref, pre_ref, c_part, cum, gain, skip,
    low_ref, dz, dy_ref, local, row_ref, dgain, dskip, gate, back, high, low, heads, sems,
):
    move = Mover(sems)
    first = [move.take(grad_hbm, grad), move.take(w_hbm, w)]
    small = [
        move.take(src, dst) for src, dst in ((cum_hbm, cum), (skip_hbm, skip), (gain_hbm, gain))
    ]
    small.append(move.take(vbc_hbm.at[:, pl.ds(INNER + NSTATE, NSTATE)], c_part))
    copies = []
    for k in range(3):
        span = pl.ds(512 * k, 512)
        copies.append(
            [
                move.take(src.at[:, span], dst.at[:, span])
                for src, dst in ((y_hbm, y_ref), (pre_hbm, pre_ref), (z_hbm, z_ref))
            ]
        )
    wait_all(first)
    low_ref[...] = grad[...].astype(bf16)
    move.give(low_ref, low_hbm)
    for k in range(6):
        cols = slice(256 * k, 256 * k + 256)
        back[:, cols] = dot_nt(low_ref[...], w[cols, :])
    wait_all(small)
    square = jnp.zeros((ROWS, 1), f32)
    cross = jnp.zeros((ROWS, 1), f32)
    for p in range(PAIRS):
        if p % 4 == 0:
            wait_all(copies[p // 4])
        cols = slice(p * LANES, (p + 1) * LANES)
        u = (y_ref[:, cols] + skip[:, cols] * silu(pre_ref[:, cols])) * silu(z_ref[:, cols])
        gate[:, cols] = u
        square = square + jnp.sum(u * u, axis=-1, keepdims=True)
        cross = cross + jnp.sum(back[:, cols] * gain[:, cols] * u, axis=-1, keepdims=True)
    scale = lax.rsqrt(square * (1.0 / INNER) + EPS)
    pull = scale * scale * scale * cross * (1.0 / INNER)
    grown = jnp.exp(cum[...])
    for p in range(PAIRS):
        cols = slice(p * LANES, (p + 1) * LANES)
        z, y = z_ref[:, cols], y_ref[:, cols]
        u, grad_p = gate[:, cols], back[:, cols]
        x = silu(pre_ref[:, cols])
        dgain[:, cols] = jnp.sum(grad_p * u * scale, axis=0, keepdims=True)
        du = grad_p * gain[:, cols] * scale - u * pull
        sig = sigmoid(z)
        dssm = du * (z * sig)
        ssm = y + skip[:, cols] * x
        dz[:, cols] = (du * ssm * (sig * (1.0 + z * (1.0 - sig)))).astype(bf16)
        dy = dssm.astype(bf16)
        dy_ref[:, cols] = dy
        gate[0:1, cols] = jnp.sum(dssm * x, axis=0, keepdims=True)
        a, b = split2(dy.astype(f32) * y)
        high[:, cols] = a
        low[:, cols] = b
        heads[:, cols] = (dssm * pair_of(grown, p)).astype(bf16)
        if p % 3 == 2:
            part = p // 3
            wide = slice(384 * part, 384 * part + 384)
            states = dot_tn(heads[:, wide], c_part[...])
            for piece in range(8):
                local[8 * part + piece] = states[48 * piece : 48 * piece + 48].astype(bf16)
    move.give(local, local_hbm)
    move.give(dz, dz_hbm)
    move.give(dy_ref, dy_hbm)
    move.give(dgain, dgain_hbm)
    mask = head_mask(INNER, 0)
    row_ref[...] = dot(high[...], mask) + dot(low[...], mask)
    move.give(row_ref, row_hbm)
    a, b = split2(jnp.broadcast_to(gate[0:1, :], (16, INNER)))
    dskip[...] = (dot(a, mask) + dot(b, mask))[0:8]
    move.give(dskip, dskip_hbm)
    move.finish()


def gate_back(grad, weight, y, z, pre, vbc, cum, gain, skip):
    outs = (
        sds((ROWS, D), bf16),
        sds((ROWS, INNER), bf16),
        sds((ROWS, INNER), bf16),
        sds((32, 48, LANES), bf16),
        sds((ROWS, LANES), f32),
        sds((1, INNER), f32),
        sds((8, LANES), f32),
    )
    wide = sds((ROWS, INNER), f32)
    wide_low = sds((ROWS, INNER), bf16)
    return moved_call(
        gate_back_kernel,
        (grad, weight, y, z, pre, vbc, cum, gain, skip),
        outs,
        (
            sds((ROWS, D), grad.dtype),
            sds((INNER, D), bf16),
            wide,
            wide,
            wide,
            sds((ROWS, NSTATE), bf16),
            sds((ROWS, LANES), f32),
            sds((1, INNER), f32),
            sds((1, INNER), f32),
            *outs,
            wide,
            wide,
            wide_low,
            wide_low,
            wide_low,
        ),
        24,
        flops=2 * ROWS * INNER * (D + LANES),
        moved=12_000_000,
        name="gate_back",
    )


def early_grads_kernel(core_ref, normed_ref, dz_ref, gated_ref, low_ref, keep_ref, send_ref):
    core = core_ref[0]
    normed_t = jnp.transpose(normed_ref[...])
    gated_t = jnp.transpose(gated_ref[...])
    for out_ref, side in ((keep_ref, core), (send_ref, 1 - core)):
        for k in range(2):
            col = pl.multiple_of((2 * k + side) * 384, LANES)
            total = dot(normed_t, dz_ref[:, pl.ds(col, 384)])
            for w in range(4):
                for rb in range(4):
                    row = 192 * w + 48 * rb
                    out_ref[w, 4 * rb + k] = total[row : row + 48].astype(bf16)
        col = pl.multiple_of(side * 384, LANES)
        total = dot(gated_t, low_ref[:, pl.ds(col, 384)])
        for k in range(2):
            for w in range(4):
                for rb in range(4):
                    row = 384 * w + 192 * k + 48 * rb
                    out_ref[w, 4 * rb + 2 + k] = total[row : row + 48].astype(bf16)


def early_grads(core, normed, dz, gated, low):
    shape = sds((4, 16, 48, 384), bf16)
    whole = pl.BlockSpec(memory_space=pltpu.VMEM)
    return call(
        early_grads_kernel,
        (shape, shape),
        in_specs=[pl.BlockSpec(memory_space=pltpu.SMEM)] + [whole] * 4,
        out_specs=[whole] * 2,
        flops=4 * ROWS * INNER * D,
        moved=7_000_000,
        name="early_grads",
    )(core, normed, dz, gated, low)


def within_back_kernel(vbc_ref, dy_ref, cum_ref, state_ref, dv_ref, dbc_ref, score, pile):
    b_part = vbc_ref[:, INNER : INNER + NSTATE]
    c_part = vbc_ref[:, INNER + NSTATE :]
    keep = iota((ROWS, ROWS), 0) <= iota((ROWS, ROWS), 1)
    score[...] = jnp.where(keep, dot_nt(b_part, c_part), 0.0)
    pile[...] = jnp.zeros_like(pile)
    cum = cum_ref[...]
    cum_t = jnp.transpose(cum)
    grown = jnp.exp(cum)
    left = iota((LANES, LANES), 1) < HDIM
    left_all = iota((ROWS, LANES), 1) < HDIM
    dc = jnp.zeros((ROWS, NSTATE), f32)
    for p in range(PAIRS):
        cols = slice(p * LANES, (p + 1) * LANES)
        values, dy = vbc_ref[:, cols], dy_ref[:, cols]
        tops, lows = [], []
        for side, h in enumerate((2 * p, 2 * p + 1)):
            col, row = cum[:, h : h + 1], cum_t[h : h + 1, :]
            mine = left_all if side == 0 else jnp.logical_not(left_all)
            own = jnp.where(mine, values.astype(f32), 0.0).astype(bf16)
            top = jnp.exp(jnp.minimum(row - col[0:LANES], 0.0))
            low = jnp.exp(jnp.minimum(row[:, LANES:] - col[LANES:], 0.0))
            tops.append(dot((top * score[0:LANES, :]).astype(bf16), dy))
            lows.append(dot((low * score[LANES:, LANES:]).astype(bf16), dy[LANES:]))
            pile[0:LANES, :] += top * dot_nt(own[0:LANES], dy)
            pile[LANES:, LANES:] += low * dot_nt(own[LANES:], dy[LANES:])
        dv_ref[0:LANES, cols] = jnp.where(left, tops[0], tops[1])
        dv_ref[LANES:, cols] = jnp.where(left, lows[0], lows[1])
        lifted = (dy.astype(f32) * pair_of(grown, p)).astype(bf16)
        dc = dc + dot(lifted, state_ref[cols, :])
    dscore = jnp.where(keep, pile[...], 0.0).astype(bf16)
    dbc_ref[:, 0:NSTATE] = dot(dscore, c_part)
    dbc_ref[:, NSTATE:] = dc + dot_tn(dscore, b_part)


def within_back(vbc, dy, cum, states):
    return call(
        within_back_kernel,
        (sds((ROWS, INNER), f32), sds((ROWS, 2 * NSTATE), f32)),
        scratch=[pltpu.VMEM((ROWS, ROWS), f32), pltpu.VMEM((ROWS, ROWS), f32)],
        flops=2 * HEADS * ROWS * ROWS * LANES * 6,
        moved=4_000_000,
        name="within_back",
    )(vbc, dy, cum, states)


def conv_back_kernel(
    later_hbm, state_hbm, dv_hbm, dy_hbm, vbc_hbm, pre_hbm, cin_hbm, edge_hbm, taps_hbm, skip_hbm,
    cum_hbm, step_hbm, dt_hbm, dbc_hbm, row_hbm, decay_hbm, dtb_hbm,
    pg_hbm, edge_grad_hbm, param_hbm, ddt_hbm, vec_hbm,
    later, state, dv_ref, dy, vbc, pre_ref, cin, edge, taps, skip,
    cum, step, dt, dbc, row_ref, decay, dtb,
    pg, edge_grad, param, ddt_ref, vec,
    ext_in, ext_out, v_high, v_low, x_high, x_low, s_high, s_low, sums, sems,
):
    move = Mover(sems)
    small = [
        move.take(src, dst)
        for src, dst in (
            (cum_hbm, cum), (step_hbm, step), (later_hbm, later), (taps_hbm, taps), (skip_hbm, skip),
            (edge_hbm, edge), (state_hbm, state), (dbc_hbm, dbc),
        )
    ]
    small.append(move.take(vbc_hbm.at[:, pl.ds(INNER, NSTATE)], vbc.at[:, pl.ds(INNER, NSTATE)]))
    chunks = [(0, 512), (512, 512), (1024, 512)]
    copies = []
    for start, count in chunks:
        span = pl.ds(start, count)
        copies.append(
            [
                move.take(src.at[:, span], dst.at[:, span])
                for src, dst in (
                    (dv_hbm, dv_ref), (dy_hbm, dy), (vbc_hbm, vbc), (pre_hbm, pre_ref), (cin_hbm, cin),
                )
            ]
        )
    span = pl.ds(INNER, 256)
    copies.append([move.take(src.at[:, span], dst.at[:, span]) for src, dst in ((pre_hbm, pre_ref), (cin_hbm, cin))])
    last = [
        move.take(src, dst)
        for src, dst in ((dt_hbm, dt), (row_hbm, row_ref), (decay_hbm, decay), (dtb_hbm, dtb))
    ]
    wait_all(small)
    step_all = step[...]
    tail = jnp.exp(cum[ROWS - 1 : ROWS] - cum[...])
    b_part = vbc[:, INNER : INNER + NSTATE]

    def conv_part(block, dout):
        cols = slice(block * LANES, (block + 1) * LANES)
        pre = pre_ref[:, cols]
        sig = sigmoid(pre)
        ds = dout * (sig * (1.0 + pre * (1.0 - sig)))
        ext_out[block, 0:8] = jnp.zeros((8, LANES), f32)
        ext_out[block, 8 : 8 + ROWS] = ds
        ext_out[block, ROWS + 8 :] = jnp.zeros((8, LANES), f32)
        ext_in[block, 0:8] = edge[:, cols]
        ext_in[block, 8 : 8 + ROWS] = cin[:, cols]
        grad = taps[3:4, cols] * ds
        before = jnp.zeros((8, LANES), f32)
        param[3:4, cols] = jnp.sum(ds * cin[:, cols], axis=0, keepdims=True)
        for tap in range(WIDTH - 1):
            ahead = WIDTH - 1 - tap
            weight = taps[tap : tap + 1, cols]
            grad = grad + weight * ext_out[block, 8 + ahead : 8 + ahead + ROWS]
            before = before + weight * ext_out[block, ahead : ahead + 8]
            param[tap : tap + 1, cols] = jnp.sum(
                ds * ext_in[block, 5 + tap : 5 + tap + ROWS], axis=0, keepdims=True
            )
        param[4:5, cols] = jnp.sum(ds, axis=0, keepdims=True)
        param[5:8, cols] = jnp.zeros((3, LANES), f32)
        pg[:, cols] = grad
        edge_grad[:, cols] = before

    acc_b = jnp.zeros((ROWS, NSTATE), f32)
    for p in range(PAIRS):
        if p % 4 == 0:
            wait_all(copies[p // 4])
        cols = slice(p * LANES, (p + 1) * LANES)
        tail_p = pair_of(tail, p)
        later_p = later[cols, :]
        value = vbc[:, cols].astype(f32)
        acc_b = acc_b + dot((value * tail_p).astype(bf16), later_p)
        from_state = tail_p * dot_nt(b_part, later_p)
        dv = dv_ref[:, cols] + from_state
        v_high[:, cols], v_low[:, cols] = split2(value * dv)
        x_high[:, cols], x_low[:, cols] = split2(silu(pre_ref[:, cols]) * dv)
        sums[0:1, cols] = jnp.sum(value * from_state, axis=0, keepdims=True)
        s_high[cols, :], s_low[cols, :] = split2(later_p.astype(f32) * state[cols, :].astype(f32))
        conv_part(p, pair_of(step_all, p) * dv + skip[:, cols] * dy[:, cols].astype(f32))
        if p % 4 == 3:
            span = pl.ds(512 * (p // 4), 512)
            move.give(pg.at[:, span], pg_hbm.at[:, span])
    wait_all(copies[3])
    conv_part(PAIRS, dbc[:, 0:NSTATE] + acc_b)
    conv_part(PAIRS + 1, dbc[:, NSTATE:])
    span = pl.ds(INNER, 256)
    move.give(edge_grad, edge_grad_hbm)
    move.give(pg.at[:, span], pg_hbm.at[:, span])
    move.give(param, param_hbm)
    wait_all(last)
    mask = head_mask(INNER, 0)
    total_v = dot(v_high[...], mask) + dot(v_low[...], mask)
    total_x = dot(x_high[...], mask) + dot(x_low[...], mask)
    high, low = split2(jnp.broadcast_to(sums[0:1, :], (16, INNER)))
    total_t = dot(high, mask) + dot(low, mask)
    ones = jnp.ones((16, NSTATE), bf16)
    high, low = split2(dot_nt(ones, s_high[...]) + dot_nt(ones, s_low[...]))
    total_s = dot(high, mask) + dot(low, mask)
    inside = iota((ROWS, LANES), 1) < HEADS
    raw = dt[...] + dtb[...]
    rate = jnp.exp(decay[...])
    log_decay = -step_all * rate
    whole = total_t[0:1] + jnp.exp(cum[ROWS - 1 : ROWS]) * total_s[0:1]
    dlog = running_sum(row_ref[...] - total_v, True) + whole
    dstep = total_x - dlog * rate
    ddt = jnp.where(inside, dstep * sigmoid(raw), 0.0)
    ddt_ref[...] = ddt.astype(bf16)
    vec[0:1] = jnp.sum(jnp.where(inside, dlog * log_decay, 0.0), axis=0, keepdims=True)
    vec[1:2] = jnp.sum(ddt, axis=0, keepdims=True)
    vec[2:8] = jnp.zeros((6, LANES), f32)
    move.give(ddt_ref, ddt_hbm)
    move.give(vec, vec_hbm)
    move.finish()


def conv_back(later, states, dv, dy, vbc, pre, cin, edge, taps, skip, cum, step, dt, dbc, row, decay, dtb):
    outs = (
        sds((ROWS, CONV), f32),
        sds((8, CONV), f32),
        sds((8, CONV), f32),
        sds((ROWS, LANES), bf16),
        sds((8, LANES), f32),
    )
    wide_low = sds((ROWS, INNER), bf16)
    blocks = CONV // LANES
    ins = (later, states, dv, dy, vbc, pre, cin, edge, taps, skip, cum, step, dt, dbc, row, decay, dtb)
    return moved_call(
        conv_back_kernel,
        ins,
        outs,
        (
            *(sds(a.shape, a.dtype) for a in ins),
            *outs,
            sds((blocks, ROWS + 8, LANES), f32),
            sds((blocks, ROWS + 16, LANES), f32),
            wide_low,
            wide_low,
            wide_low,
            wide_low,
            sds((INNER, NSTATE), bf16),
            sds((INNER, NSTATE), bf16),
            sds((8, INNER), f32),
        ),
        44,
        flops=6 * ROWS * INNER * NSTATE,
        moved=12_000_000,
        name="conv_back",
    )


def finish_kernel(
    core_ref, pg_hbm, next_hbm, dz_hbm, ddt_hbm, w_hbm, wd_hbm, x_hbm, gain_hbm, grad_hbm,
    normed_hbm, dgain_out_hbm, param_hbm, vec_hbm, dskip_hbm,
    out_hbm, keep_hbm, send_hbm,
    pg, following, dz, ddt, w, wd, x_ref, gain, grad, normed, dgain_out, param, vec_ref, dskip,
    out, keep, send, low, small, sems,
):
    core = core_ref[0]
    move = Mover(sems)
    first = [move.take(pg_hbm, pg), move.take(next_hbm, following)]
    spans = [pl.ds(INNER, CONV), pl.ds(0, INNER)]
    weights = [move.take(w_hbm.at[:, span], w.at[:, span]) for span in spans]
    second = [move.take(src, dst) for src, dst in ((dz_hbm, dz), (ddt_hbm, ddt), (wd_hbm, wd))]
    third = [move.take(src, dst) for src, dst in ((x_hbm, x_ref), (gain_hbm, gain), (grad_hbm, grad))]
    fourth = [
        move.take(src, dst)
        for src, dst in (
            (normed_hbm, normed), (dgain_out_hbm, dgain_out), (param_hbm, param), (vec_hbm, vec_ref), (dskip_hbm, dskip),
        )
    ]
    wait_all(first)
    low[0 : ROWS - 16] = pg[0 : ROWS - 16].astype(bf16)
    last = pg[ROWS - 16 :]
    low[ROWS - 16 :] = jnp.concatenate([last[0:8], last[8:16] + following[...]]).astype(bf16)
    weights[0].wait()
    back = dot_nt(low[...], w[:, INNER : INNER + CONV])
    wait_all(second)
    back = back + dot_nt(ddt[...], wd[...])
    weights[1].wait()
    back = back + dot_nt(dz[...], w[:, 0:INNER])
    wait_all(third)
    x = x_ref[...].astype(f32)
    scale = lax.rsqrt(jnp.mean(x * x, axis=-1, keepdims=True) + EPS)
    dgain_in = jnp.sum(back * x * scale, axis=0, keepdims=True)
    scaled = back * gain[...]
    pull = scale * scale * scale * jnp.mean(scaled * x, axis=-1, keepdims=True)
    out[...] = grad[...].astype(f32) + scaled * scale - x * pull
    move.give(out, out_hbm)

    wait_all(fourth)
    small[...] = jnp.zeros_like(small)
    line = 0
    for i in range(D // LANES):
        small[line : line + 1, :] = dgain_in[:, LANES * i : LANES * i + LANES]
        line += 1
    for i in range(INNER // LANES):
        small[line : line + 1, :] = dgain_out[:, LANES * i : LANES * i + LANES]
        line += 1
    for tap in range(WIDTH + 1):
        for i in range(CONV // LANES):
            small[line : line + 1, :] = param[tap : tap + 1, LANES * i : LANES * i + LANES]
            line += 1
    vec = vec_ref[...]
    lane = iota((8, LANES), 1)
    decay = jnp.where(lane < HEADS, jnp.broadcast_to(vec[0:1], (8, LANES)), 0.0)
    dtb = jnp.where(lane < HEADS, jnp.broadcast_to(vec[1:2], (8, LANES)), 0.0)
    skip = jnp.where(lane < HEADS, dskip[...], 0.0)
    joined = decay + pltpu.roll(dtb, HEADS, 1) + pltpu.roll(skip, 2 * HEADS, 1)
    small[line : line + 1, :] = joined[0:1]

    normed_t = jnp.transpose(normed[...])

    def place(out_ref, k, lanes, total):
        for shard in range(4):
            for rb in range(4):
                row = 192 * shard + 48 * rb
                out_ref[shard, 4 * rb + k, :, lanes] = total[row : row + 48].astype(bf16)

    for out_ref, out_ref_hbm, side in ((send, send_hbm, 1 - core), (keep, keep_hbm, core)):
        for k in range(3):
            col = pl.multiple_of((2 * k + side) * 256, LANES)
            place(out_ref, k, slice(0, 256), dot(normed_t, low[:, pl.ds(col, 256)]))

        @pl.when(side == 0)
        def _(out_ref=out_ref):
            place(out_ref, 3, slice(0, 256), dot(normed_t, low[:, 1536:1792]))

        @pl.when(side == 1)
        def _(out_ref=out_ref):
            place(out_ref, 3, slice(0, 128), dot(normed_t, ddt[...]))
            for shard in range(4):
                for rb in range(4):
                    if rb < 2:
                        block = small[48 * rb : 48 * rb + 48, :]
                    else:
                        block = jnp.zeros((48, LANES), f32)
                    out_ref[shard, 4 * rb + 3, :, 128:256] = block.astype(bf16)

        move.give(out_ref, out_ref_hbm)
    move.finish()


def finish(core, pg, following, dz, ddt, weight, weight_dt, x, gain, grad, normed, dgain_out, param, vec, dskip):
    pieces = sds((4, 16, 48, 256), bf16)
    outs = (sds((ROWS, D), f32), pieces, pieces)
    ins = (pg, following, dz, ddt, weight, weight_dt, x, gain, grad, normed, dgain_out, param, vec, dskip)
    return moved_call(
        finish_kernel,
        (core, *ins),
        outs,
        (
            *(sds(a.shape, a.dtype) for a in ins),
            *outs,
            sds((ROWS, CONV), bf16),
            sds((96, LANES), f32),
        ),
        24,
        smem=1,
        flops=2 * ROWS * D * (PROJ + CONV),
        moved=16_000_000,
        name="finish",
    )


def adam_step(weight, moment, second, gradient, learn_rate, weight_decay):
    new_moment = 0.9 * moment + 0.1 * gradient
    new_second = 0.95 * second + 0.05 * gradient * gradient
    corrected = new_moment / (1.0 - 0.9**STEP) / (jnp.sqrt(new_second / (1.0 - 0.95**STEP)) + 1e-08)
    return (new_moment, new_second, weight - learn_rate * (corrected + weight_decay * weight))


def adam_kernel(
    core_ref, early_own, early_other, late_own, late_other, in_w, in_m, in_v, out_w, out_m, out_v, *refs
):
    in_outs, out_outs, token = refs[-7:-4], refs[-4:-1], refs[-1]
    token[...] = jnp.zeros_like(token)
    first = core_ref[0] == 0

    def sides(own, other, k):
        a, b = own[0, k].astype(f32), other[0, k].astype(f32)
        return jnp.where(first, a, b), jnp.where(first, b, a)

    def update(ins, outs, spot, grad, rate):
        new_m, new_v, new_w = adam_step(*(ref[spot] for ref in ins), grad, rate, 0.1)
        for out, new in zip(outs, (new_w, new_m, new_v), strict=True):
            out[spot] = new

    def update_in(col, width, grad):
        update((in_w, in_m, in_v), in_outs, (0, slice(None), slice(col, col + width)), grad, 0.03)

    for k in range(4):
        for side, grad in enumerate(sides(early_own, early_other, k)):
            if k < 2:
                update_in(384 * (2 * k + side), 384, grad)
            else:
                spot = (0, k - 2, slice(None), slice(384 * side, 384 * side + 384))
                update((out_w, out_m, out_v), out_outs, spot, grad, 0.02)
        for side, grad in enumerate(sides(late_own, late_other, k)):
            if 2 * k + side < 7:
                update_in(INNER + 256 * (2 * k + side), 256, grad)
            else:
                update_in(INNER + CONV, HEADS, grad[:, 0:HEADS])


def adam(core, early, early_at, late, late_at, in_state, out_state, layer, before):
    rows = 48
    in_block = pl.BlockSpec((1, rows, PROJ), lambda r: (layer, r, 0))
    out_block = pl.BlockSpec((1, 2, rows, D), lambda r: (layer, 0, r, 0))
    early_block = pl.BlockSpec((1, 4, rows, 384), lambda r: (r, 0, 0, early_at))
    late_block = pl.BlockSpec((1, 4, rows, 256), lambda r: (r, 0, 0, late_at))
    in_shape = sds((2, 192, PROJ), f32)
    out_shape = sds((2, 2, 192, D), f32)
    held = () if before is None else tuple(before[:6])
    return call(
        adam_kernel,
        (in_shape,) * 3 + (out_shape,) * 3 + (sds((8, LANES), bf16),),
        grid=(192 // rows,),
        in_specs=[pl.BlockSpec(memory_space=pltpu.SMEM)]
        + [early_block] * 2
        + [late_block] * 2
        + [in_block] * 3
        + [out_block] * 3
        + [pl.BlockSpec(memory_space=pl.ANY)] * len(held),
        out_specs=[in_block] * 3 + [out_block] * 3 + [pl.BlockSpec((8, LANES), lambda r: (0, 0))],
        input_output_aliases={11 + n: n for n in range(len(held))},
        moved=24_000_000,
        name="adam",
    )(core, *early, *late, *in_state, *out_state, *held)


def next_in_sequence(rows, step):
    route = [(i, i + step) for i in range(32) if 0 <= i + step < 32]
    return lax.ppermute(rows, PLANE, route)


def exchange(blocks):
    return lax.all_to_all(blocks, PLANE, 0, 0, tiled=True)


def turned(block, axis, step):
    return lax.ppermute(block, axis, [(i, (i + step) % 4) for i in range(4)])


def swapped(block):
    return lax.ppermute(block, "core", [(0, 1), (1, 0)])


def gather_start(shard, rider=None):
    half = lax.dynamic_slice_in_dim(shard, 96 * lax.axis_index("core"), 96, 0).astype(bf16)
    if rider is not None:
        half = jnp.concatenate([half, rider])
    return turned(half, "wt", 1), turned(half, "wt", -1)


def gather_far(before, after):
    return turned(before[:48], "wt", 1), turned(after[48:], "wt", -1)


def all_pieces(shard, mine):
    return [shard, *mine, *[swapped(piece) for piece in mine]]


def tie(*values):
    return lax.optimization_barrier(values)


def paired(keep, send):
    return (keep.astype(f32) + swapped(send).astype(f32)).astype(bf16)


def summed(parts):
    return jnp.sum(parts.astype(f32), axis=0).astype(bf16)


def over_wt(pieces):
    return lax.psum_scatter(pieces, "wt", scatter_dimension=0, tiled=True)[0]


def over_plane(part):
    return summed(lax.all_to_all(part, ("x", "z"), 0, 0, tiled=True))


def spread(piece):
    pieces = jnp.broadcast_to(piece[None], (16, *piece.shape))
    own = lax.all_to_all(pieces, ("x", "z"), 0, 0, tiled=True).reshape(4, 4, *piece.shape)
    return own, swapped(own)


def shards(
    tokens, in_w, in_m, in_v, out_w, out_m, out_v, small_params, small_m, small_v, cotangent
):
    core = lax.axis_index("core").astype(jnp.int32).reshape(1)
    tokens = tokens[0]
    cotangent = cotangent[0]
    in_low, out_low = in_w.astype(bf16), out_w.astype(bf16)
    rider = jnp.pad(small_params.astype(bf16), ((0, 6), (0, PROJ - VEC // 4)))
    near = gather_start(in_w[0], rider)
    far = gather_far(*near)
    *far, out_now = tie(*far, out_low[0])
    pieces = [all_pieces(in_low[0], (*near, *far)), None]
    place = jnp.stack([lax.axis_index("wt"), lax.axis_index("core")]).astype(jnp.int32)
    out_full = [lax.all_gather(out_now, "wt", axis=0, tiled=True), None]
    riders = jnp.stack([rider, near[1][96:], far[1][48:], near[0][96:]])
    riders = riders[lax.rem(jnp.arange(4) + 4 - lax.axis_index("wt"), 4)]
    small_full = jnp.swapaxes(riders[:, :2, : VEC // 4], 0, 1).reshape(2, VEC).astype(f32)

    def heads_row(first):
        return jnp.pad(small_full[:, first : first + HEADS], ((0, 0), (0, LANES - HEADS)))

    gain_in = small_full[:, :D]
    gain_out = small_full[:, D : D + INNER]
    taps = small_full[:, 2304:9472].reshape(2, WIDTH, CONV)
    bias = small_full[:, 9472:11264]
    decay = heads_row(11264)
    dtb = heads_row(11264 + HEADS)
    skip = jnp.repeat(small_full[:, 11264 + 2 * HEADS : VEC], HDIM, axis=1)

    hidden = tokens
    saved = []
    for layer in range(2):
        row = slice(layer, layer + 1)
        edge = next_in_sequence(hidden[ROWS - 8 :], 1)
        weight, weight_dt, normed, z, cin, dt = project(place, hidden, gain_in[row], pieces[layer])
        if layer == 0:
            normed, shard = tie(normed, in_w[1])
            near = gather_start(shard)
        pre, edge_in, vbc, cum, step, pay = conv_states(
            edge, gain_in[row], weight, cin, dt, taps[layer], bias[row], decay[row], dtb[row]
        )
        slices = exchange(pay)
        yw = within(vbc, cum)
        if layer == 0:
            slices, *near = tie(slices, *near)
            far = gather_far(*near)
        scanned, chain = scan_states(slices)
        states = exchange(scanned)
        if layer == 0:
            states, yw, *far = tie(states, yw, *far)
        states = states.reshape(INNER, NSTATE)
        after, y, gated = output_part(
            yw, vbc, cum, pre, z, states, hidden, out_full[layer], gain_out[row], skip[row]
        )
        saved.append(
            (hidden, weight, weight_dt, normed, z, cin, dt, pre, edge_in, vbc, cum, step, chain, states, y, gated)
        )
        hidden = after
        if layer == 0:
            after, out_now = tie(after, out_low[1])
            hidden = after
            pieces[1] = all_pieces(in_low[1], (*near, *far))
            out_full[1] = lax.all_gather(out_now, "wt", axis=0, tiled=True)

    grad = cotangent
    early_part, late_part = [None, None], [None, None]
    for layer in (1, 0):
        row = slice(layer, layer + 1)
        start, weight, weight_dt, normed, z, cin, dt, pre, edge_in, vbc, cum, step, chain, states, y, gated = saved[layer]
        low, dz, dy, local, rows_sum, dgain_out, dskip = gate_back(
            grad, out_full[layer], y, z, pre, vbc, cum, gain_out[row], skip[row]
        )
        slices = exchange(local)
        keep, send = early_grads(core, normed, dz, gated, low)
        dv, dbc = within_back(vbc, dy, cum, states)
        slices, keep, send, dv, dbc = tie(slices, keep, send, dv, dbc)
        scanned = scan_back(slices, chain)
        later = exchange(scanned)
        early = paired(keep, send)
        later, early = tie(later, early)
        later = later.reshape(INNER, NSTATE)
        early_part[layer] = over_wt(early)
        if layer == 0:
            upper = jnp.concatenate([early_part[1], late_part[1]], axis=2)
            later, upper = tie(later, upper)
            upper_sum = over_plane(upper)
        pg, edge_grad, param, ddt, vec = conv_back(
            later, states, dv, dy, vbc, pre, cin, edge_in, taps[layer], skip[row],
            cum, step, dt, dbc, rows_sum, decay[row], dtb[row],
        )
        following = next_in_sequence(edge_grad, -1)
        if layer == 0:
            pg, upper_sum = tie(pg, upper_sum)
        grad, keep, send = finish(
            core, pg, following, dz, ddt, weight, weight_dt, start, gain_in[row], grad, normed,
            dgain_out, param, vec, dskip,
        )
        late = paired(keep, send)
        late_part[layer] = over_wt(late)

    early_sum = over_plane(early_part[0])
    first_all = spread(jnp.concatenate([upper_sum[:, :384], early_sum, upper_sum[:, 384:]], axis=1))
    split = lambda a: a.reshape(2, 2, 192, D)
    in_state, out_state = (in_w, in_m, in_v), (split(out_w), split(out_m), split(out_v))
    news = adam(core, first_all, 0, first_all, 3, in_state, out_state, 1, None)
    last_part, first_all = tie(late_part[0], first_all)
    last_all = spread(over_plane(last_part) + news[6][0, 0])
    news = adam(core, first_all, 1, last_all, 0, in_state, out_state, 0, news)
    small_total = jnp.stack(
        [
            jnp.where(core[0] == 0, other, own)[0:2, 3, :, at + LANES : at + 2 * LANES].reshape(96 * LANES)[:VEC]
            for (own, other), at in ((last_all, 0), (first_all, 768))
        ]
    )
    width = VEC // 4
    small_total = lax.dynamic_slice_in_dim(
        small_total.astype(f32), lax.axis_index("wt") * width, width, 1
    )
    new_small = adam_step(small_params, small_m, small_v, small_total, 0.2, 0.0)
    return (
        hidden[None],
        grad[None],
        news[1],
        news[2],
        news[0],
        news[4].reshape(2, 384, D),
        news[5].reshape(2, 384, D),
        news[3].reshape(2, 384, D),
        *new_small,
    )


def solution(mesh):
    fine = Mesh(mesh.devices.reshape(4, 4, 2, 4), ("x", "z", "core", "wt"))
    rows = P("wt", PLANE, None)
    held = P(None, "wt", None)
    flat = P(None, "wt")
    return jax.shard_map(
        shards,
        mesh=fine,
        in_specs=(rows, held, held, held, held, held, held, flat, flat, flat, rows),
        out_specs=(rows, rows, held, held, held, held, held, held, flat, flat, flat),
        check_vma=False,
    )
```
